128 devices in a mesh: user: 16 (over z, x), item: 8 (over y, core).
Axes of the slice: x: 4, y: 4, z: 4, core: 2. Of those that a mesh axis runs over, the one named last changes fastest.
Arguments:
- cand_ids: int32 [128, 1024], P(('user', 'item')), may hold values from 0 to 524287, as said below
- hist_ids: int32 [128, 1024], P(('user', 'item')), may hold values from 0 to 524287, as said below
- hist_len: int32 [128], P(('user', 'item')), may hold values from 1 to 1024, as said below
- teacher: float32 [128, 1024], P(('user', 'item')), may hold values from -16 to 16
- table: bfloat16 [524288, 256], P(('user', 'item')), may hold values from -6 to 6
- w_query: bfloat16 [256, 256], replicated, may hold values from -0.375 to 0.375
- w_key: bfloat16 [256, 256], replicated, may hold values from -0.375 to 0.375
- w_value: bfloat16 [256, 256], replicated, may hold values from -0.375 to 0.375
Outputs:
- grad_table: float32 [524288, 256], P(('user', 'item'))
The draws below stay inside these ranges and needn't reach their ends.
Inputs may be any that keep to these rules, and one draw needn't show every extreme that they name: `hist_ids`: ids are owned in blocks of 4096: id // 4096 is the owning device in the order of user+item. Of the 2048 candidate and history ids of one device's users together, at most 40 fall in one owner's block; in every draw some owner receives exactly 40 from every device. `cand_ids`: the same bound as for hist_ids holds for candidate and history ids together. `hist_len`: some user's history has exactly 1024 behaviours; history slots at or beyond a user's length are ignored.
All inputs are finite; a program needn't handle non-finite values.
Results may differ from the reference program's by a relative error of at most 0.022.
Values may be sent and summed in bfloat16 or wider, within the bound.
A program may use at most 64 MiB of HBM per device.

```python
import math
import jax
import jax.numpy as jnp
from jax import lax

D = 256
HEADS = 4
ROWS_DEV = 4096
USR_DEV = 1
CAND = 1024
HIST = 1024
GRAD_SCALE = 1024
USERS = 128
VOCAB = 524288


def owner_table(key):
    devs = USERS // USR_DEV
    slots = USR_DEV * (CAND + HIST)
    mean = slots // devs
    high = 5 * mean // 2
    low = mean // 2
    busy_count = devs // 4
    key_hot, key_rest = jax.random.split(key)
    hot = jax.random.randint(key_hot, (), 0, devs)

    def one_device(dev_key):
        key_busy, key_order, key_local = jax.random.split(dev_key, 3)
        offsets = jax.random.permutation(key_busy, devs - 1) + 1
        chosen = jnp.concatenate([jnp.zeros((1,), jnp.int32), offsets[:busy_count - 1].astype(jnp.int32)])
        busy = (hot + chosen) % devs
        flags = jnp.zeros((devs,), jnp.int32).at[busy].set(1)
        counts = jnp.where(flags == 1, high, low).astype(jnp.int32)
        starts = jnp.cumsum(counts) - counts
        position = jnp.arange(slots, dtype=jnp.int32)
        owner = jnp.sum((starts[None, :] <= position[:, None]).astype(jnp.int32), axis=1) - 1
        owner = jax.random.permutation(key_order, owner)
        local = jax.random.randint(key_local, (slots,), 0, ROWS_DEV)
        return (owner * ROWS_DEV + local).astype(jnp.int32).reshape(USR_DEV, CAND + HIST)
    every = jax.vmap(one_device)(jax.random.split(key_rest, devs))
    return every.reshape(USERS, CAND + HIST)


def draw_cand_ids(key, part):
    return owner_table(key)[:, :CAND]


def draw_hist_ids(key, part):
    return owner_table(key)[:, CAND:]


def draw_hist_len(key, part):
    key = jax.random.fold_in(key, 7)
    key_len, key_top = jax.random.split(key)
    lengths = jax.random.randint(key_len, (USERS,), 1, HIST // 2 + 1)
    longest = jax.random.randint(key_top, (), 0, USERS)
    return jnp.where(jnp.arange(USERS) == longest, HIST, lengths).astype(jnp.int32)


def level_of(rng, shape, cuts, least, high):
    loudness, own = 1.0, jax.random.fold_in(rng, 6)
    for dim, blocks in cuts:
        heights = jnp.exp(jax.random.uniform(jax.random.fold_in(own, dim), (blocks,), jnp.float32, least / len(cuts), high / len(cuts)))
        loudness = loudness * jnp.repeat(heights, shape[dim] // blocks).reshape([-1 if axis == dim else 1 for axis in range(len(shape))])
    return loudness


def scatter_about(key, shape, scale, reach, pieces=(), held_as=jnp.bfloat16):
    values = scale * jax.random.normal(key, shape, jnp.float32)
    if pieces:
        values = values * level_of(key, shape, pieces, -0.22, 0.18)
    return jnp.clip(values, -reach, reach).astype(held_as)


def setup_inputs(seed: int = 0) -> dict:
    key_list = jax.random.split(jax.random.key(seed), 9)
    cand_ids = draw_cand_ids(jax.random.fold_in(key_list[8], 71), 0)
    hist_ids = draw_hist_ids(jax.random.fold_in(key_list[8], 71), 0)
    hist_len = draw_hist_len(jax.random.fold_in(key_list[8], 71), 0)
    teacher = scatter_about(key_list[3], (USERS, CAND), 3.0, 16.0, ((0, 128),), jnp.float32)
    table = scatter_about(key_list[4], (VOCAB, D), 1.0, 6.0, ((0, 128),))
    w_query = scatter_about(key_list[5], (D, D), D ** -0.5, 0.375)
    w_key = scatter_about(key_list[6], (D, D), D ** -0.5, 0.375)
    w_value = scatter_about(key_list[7], (D, D), D ** -0.5, 0.375)
    return dict(cand_ids=cand_ids, hist_ids=hist_ids, hist_len=hist_len, teacher=teacher, table=table, w_query=w_query, w_key=w_key, w_value=w_value)


def project(hist_full, w_key, w_value):
    hist_half = hist_full.astype(jnp.bfloat16)
    keys = jnp.dot(hist_half, w_key, preferred_element_type=jnp.float32).astype(jnp.bfloat16)
    values = jnp.dot(hist_half, w_value, preferred_element_type=jnp.float32).astype(jnp.bfloat16)
    return (keys, values)

def block_loss(cand_rows, keys, values, length, target, w_query):
    cand_half = cand_rows.astype(jnp.bfloat16)
    query = jnp.dot(cand_half, w_query, preferred_element_type=jnp.float32).astype(jnp.bfloat16)
    q_heads = query.reshape(query.shape[0], HEADS, -1)
    k_heads = keys.reshape(keys.shape[0], HEADS, -1)
    v_heads = values.reshape(values.shape[0], HEADS, -1)
    score = jnp.einsum('jhd,thd->hjt', q_heads, k_heads, preferred_element_type=jnp.float32)
    score = score / math.sqrt(q_heads.shape[2])
    live = jnp.arange(k_heads.shape[0], dtype=jnp.int32) < length
    raised = jnp.where(live[None, None, :], jnp.exp(score), 0.0)
    attn = (raised / lax.optimization_barrier(jnp.sum(raised, axis=2, keepdims=True))).astype(jnp.bfloat16)
    attended = jnp.einsum('hjt,thd->jhd', attn, v_heads, preferred_element_type=jnp.float32)
    attended = attended.reshape(attended.shape[0], -1)
    logit = lax.optimization_barrier(jnp.sum(attended * cand_rows, axis=1)) / math.sqrt(attended.shape[1])
    soft_target = jax.nn.sigmoid(target)
    return GRAD_SCALE * jnp.sum(jax.nn.softplus(logit) - soft_target * logit)

def user_grads(cand_rows, hist_rows, length, target, w_query, w_key, w_value):

    def projected(hist_full):
        return project(hist_full, w_key, w_value)
    (keys, values), proj_back = jax.vjp(projected, hist_rows.astype(jnp.float32))
    cand_count, width = cand_rows.shape
    block = min(512, cand_count)
    cand_blocks = cand_rows.astype(jnp.float32).reshape(cand_count // block, block, width)
    target_blocks = target.reshape(cand_count // block, block)

    def advance(carry, item):
        cand_part, target_part = item

        def scaled(cand_full, key_part, value_part):
            return block_loss(cand_full, key_part, value_part, length, target_part, w_query)
        loss_value, pullback = jax.vjp(scaled, cand_part, keys, values)
        grad_cand, grad_keys, grad_values = pullback(jnp.ones_like(loss_value))
        summed = (carry[0] + grad_keys.astype(jnp.float32), carry[1] + grad_values.astype(jnp.float32))
        return (summed, grad_cand)
    start = (jnp.zeros(keys.shape, jnp.float32), jnp.zeros(values.shape, jnp.float32))
    (key_total, value_total), grad_cand = lax.scan(advance, start, (cand_blocks, target_blocks))
    grad_hist, = proj_back((key_total.astype(jnp.bfloat16), value_total.astype(jnp.bfloat16)))
    return (grad_cand.reshape(cand_count, width), grad_hist)

def reference(cand_ids, hist_ids, hist_len, teacher, table, w_query, w_key, w_value):

    def advance(total, item):
        cand, hist, length, target = item
        grad_cand, grad_hist = user_grads(table[cand], table[hist], length, target, w_query, w_key, w_value)
        named = jnp.concatenate([cand, hist]).astype(jnp.int32)
        rows = jnp.concatenate([grad_cand, grad_hist], axis=0)
        return (total.at[named].add(rows), None)
    start_total = jnp.zeros(table.shape, jnp.float32)
    grad_table, unused = lax.scan(advance, start_total, (cand_ids, hist_ids, hist_len, teacher))
    return grad_table
```

```python
import math

import jax
import jax.numpy as jnp
from jax import lax
from jax.experimental import pallas as pl
from jax.experimental.pallas import tpu as pltpu
from jax.sharding import PartitionSpec as P

HEADS = 4
GRAD_SCALE = 1024


CAND = 1024
HIST = 1024
WIDTH = 256
HEAD = 64
BLOCK = 256


def dot(a, b):
    return jnp.dot(a, b, preferred_element_type=jnp.float32)


def dot_tn(a, b):
    return lax.dot_general(a, b, (((0,), (0,)), ((), ())), preferred_element_type=jnp.float32)


def dot_nt(a, b):
    return lax.dot_general(a, b, (((1,), (1,)), ((), ())), preferred_element_type=jnp.float32)


def attention_kernel(len_ref, rows_ref, teacher_ref, wq_ref, wk_ref, wv_ref, out_ref, q_s, kt_s, vt_s, vk1_s, cq_s, ee_s, xx_s, dvk_s):
    half = jnp.bfloat16
    length = len_ref[0]
    live = lax.broadcasted_iota(jnp.int32, (HIST, 128), 0) < length
    live2 = jnp.concatenate([live, live], axis=1)
    hist = jnp.where(live2, rows_ref[CAND:, :], jnp.zeros((), half))
    keys = dot(hist, wk_ref[...]).astype(half)
    values = dot(hist, wv_ref[...]).astype(half)
    kt_s[...] = keys.T
    vt_s[...] = values.T
    cand = rows_ref[:CAND, :]
    query = dot(cand, wq_ref[...]).astype(half)
    q_s[...] = query
    ones = jnp.where(live, 1.0, 0.0).astype(half)
    for h in range(HEADS):
        part = slice(h * HEAD, (h + 1) * HEAD)
        vk1_s[h] = jnp.concatenate([values[:, part], keys[:, part], ones], axis=1)
        cq_s[h] = jnp.concatenate([cand[:, part], query[:, part]], axis=1)
    dvk_s[...] = jnp.zeros_like(dvk_s)
    first = lax.broadcasted_iota(jnp.int32, (BLOCK, 128), 1) < HEAD
    scale = 1.0 / (math.sqrt(HEAD) * math.log(2.0))

    def step(jb, carry):
        here = pl.ds(pl.multiple_of(jb * BLOCK, BLOCK), BLOCK)
        logit = jnp.zeros((BLOCK, 128), jnp.float32)
        kept = []
        for h in range(HEADS):
            part = slice(h * HEAD, (h + 1) * HEAD)
            cq = cq_s[h, here, :]
            score = dot(cq[:, HEAD:], kt_s[part, :])
            worth = dot(cq[:, :HEAD], vt_s[part, :])
            top = jnp.max(score, axis=1, keepdims=True)
            raised = jnp.exp2((score - top) * scale)
            ee_s[h, :BLOCK, :] = raised.astype(half)
            ee_s[h, BLOCK:, :] = (raised * worth).astype(half)
            both = dot(ee_s[h], vk1_s[h])
            inverse = 1.0 / both[:BLOCK, 128:]
            mean = both[BLOCK:, 128:] * inverse
            plain = both[:BLOCK, :128] * inverse
            lifted = both[BLOCK:, :128] * inverse - mean * plain
            logit = logit + mean
            kept.append((inverse, mean, plain, lifted))
        logit = logit / math.sqrt(WIDTH)
        factor = (GRAD_SCALE / math.sqrt(WIDTH)) * (jax.nn.sigmoid(logit) - jax.nn.sigmoid(teacher_ref[here, :]))
        direct, turned = [], []
        for h in range(HEADS):
            inverse, mean, plain, lifted = kept[h]
            cq = cq_s[h, here, :].astype(jnp.float32)
            weight = factor * inverse
            eighth = weight * (1.0 / math.sqrt(HEAD))
            xx_s[h, :BLOCK, :] = (cq * jnp.where(first, weight, -mean * eighth)).astype(half)
            xx_s[h, BLOCK:, :] = (cq * jnp.where(first, 0.0, eighth)).astype(half)
            dvk_s[h] += dot_tn(xx_s[h], ee_s[h])
            direct.append(plain[:, :HEAD] * factor[:, :HEAD])
            turned.append((lifted[:, HEAD:] * (factor[:, HEAD:] * (1.0 / math.sqrt(HEAD)))))
        back = jnp.concatenate(turned, axis=1).astype(half)
        grad = jnp.concatenate(direct, axis=1) + dot_nt(back, wq_ref[...])
        out_ref[here, :] = grad.astype(half)
        return carry

    lax.fori_loop(0, CAND // BLOCK, step, 0)
    dv = jnp.concatenate([dvk_s[h, :HEAD, :] for h in range(HEADS)], axis=0).astype(half)
    dk = jnp.concatenate([dvk_s[h, HEAD:, :] for h in range(HEADS)], axis=0).astype(half)
    grad_hist = dot_nt(dv.T, wv_ref[...]) + dot_nt(dk.T, wk_ref[...])
    out_ref[CAND:, :] = jnp.where(live2, grad_hist, 0.0).astype(half)


def attention(rows, length, teacher, w_query, w_key, w_value):
    half = jnp.bfloat16
    space = pl.BlockSpec(memory_space=pltpu.VMEM)
    return pl.pallas_call(
        attention_kernel,
        out_shape=jax.ShapeDtypeStruct((CAND + HIST, WIDTH), half),
        in_specs=[pl.BlockSpec(memory_space=pltpu.SMEM)] + [space] * 5,
        out_specs=space,
        scratch_shapes=[
            pltpu.VMEM((CAND, WIDTH), half),
            pltpu.VMEM((WIDTH, HIST), half),
            pltpu.VMEM((WIDTH, HIST), half),
            pltpu.VMEM((HEADS, HIST, 256), half),
            pltpu.VMEM((HEADS, CAND, 128), half),
            pltpu.VMEM((HEADS, 2 * BLOCK, HIST), half),
            pltpu.VMEM((HEADS, 2 * BLOCK, 128), half),
            pltpu.VMEM((HEADS, 128, HIST), jnp.float32),
        ],
        compiler_params=pltpu.CompilerParams(vmem_limit_bytes=48 * 2**20),
        cost_estimate=pl.CostEstimate(flops=4 * 10**9, bytes_accessed=3 * 2**20, transcendentals=4 * 2**20),
        name="attention",
    )(length, rows, jnp.broadcast_to(teacher.reshape(CAND, 1), (CAND, 128)), w_query, w_key, w_value)


def body(cand_ids, hist_ids, hist_len, teacher, table, w_query, w_key, w_value):
    rows_dev, width = table.shape
    users_here, cand = cand_ids.shape
    user_count = lax.axis_size("user")
    item_count = lax.axis_size("item")
    devices = user_count * item_count
    wanted = jnp.concatenate([cand_ids, hist_ids], axis=1).reshape(-1)
    slots = wanted.shape[0]
    capacity = 5 * (slots // devices) // 2
    owner = wanted // rows_dev
    local = wanted % rows_dev
    onehot = (owner[:, None] == jnp.arange(devices, dtype=jnp.int32)[None, :]).astype(jnp.int32)
    rank = jnp.sum(jnp.cumsum(onehot, axis=0) * onehot, axis=1) - 1
    place = owner * capacity + rank
    request = jnp.zeros((devices * capacity,), jnp.int32).at[place].set(local)
    asked = lax.all_to_all(
        request.reshape(devices, capacity),
        ("user", "item"),
        split_axis=0,
        concat_axis=0,
        tiled=True,
    )
    found = table[asked]
    asked, fetched = (
        asked,
        lax.all_to_all(found, ("user", "item"), split_axis=0, concat_axis=0, tiled=True),
    )
    rows = fetched.reshape(devices * capacity, width)[place].reshape(users_here, -1, width)
    grad_flat = attention(rows.reshape(-1, width), hist_len, teacher, w_query, w_key, w_value)
    outgoing = jnp.zeros((devices * capacity, width), jnp.bfloat16).at[place].set(grad_flat)
    arrived = lax.all_to_all(
        outgoing.reshape(devices, capacity, width),
        ("user", "item"),
        split_axis=0,
        concat_axis=0,
        tiled=True,
    )
    grad_table = jnp.zeros((rows_dev, width), jnp.float32)
    return grad_table.at[asked.reshape(-1)].add(arrived.reshape(-1, width).astype(jnp.float32))


def solution(mesh):
    placed = (
        P(("user", "item"), None),
        P(("user", "item"), None),
        P(("user", "item")),
        P(("user", "item"), None),
        P(("user", "item"), None),
        P(),
        P(),
        P(),
    )
    return jax.shard_map(
        body, mesh=mesh, in_specs=placed, out_specs=P(("user", "item"), None), check_vma=False
    )
```

```python
import math

import jax
import jax.numpy as jnp
from jax import lax
from jax.experimental import pallas as pl
from jax.experimental.pallas import tpu as pltpu
from jax.sharding import PartitionSpec as P

HEADS = 4
GRAD_SCALE = 1024


CAND = 1024
HIST = 1024
WIDTH = 256
HEAD = 64
BLOCK = 256


def dot(a, b):
    return jnp.dot(a, b, preferred_element_type=jnp.float32)


def dot_tn(a, b):
    return lax.dot_general(a, b, (((0,), (0,)), ((), ())), preferred_element_type=jnp.float32)


def dot_nt(a, b):
    return lax.dot_general(a, b, (((1,), (1,)), ((), ())), preferred_element_type=jnp.float32)


def attention_kernel(len_ref, rows_ref, teacher_ref, wq_ref, wk_ref, wv_ref, out_ref, q_s, kt_s, vt_s, vk1_s, cq_s, ee_s, xx_s, dvk_s):
    half = jnp.bfloat16
    length = len_ref[0]
    live = lax.broadcasted_iota(jnp.int32, (HIST, 128), 0) < length
    live2 = jnp.concatenate([live, live], axis=1)
    hist = jnp.where(live2, rows_ref[CAND:, :], jnp.zeros((), half))
    keys = dot(hist, wk_ref[...]).astype(half)
    values = dot(hist, wv_ref[...]).astype(half)
    kt_s[...] = keys.T
    vt_s[...] = values.T
    cand = rows_ref[:CAND, :]
    query = dot(cand, wq_ref[...]).astype(half)
    q_s[...] = query
    ones = jnp.where(live, 1.0, 0.0).astype(half)
    for h in range(HEADS):
        part = slice(h * HEAD, (h + 1) * HEAD)
        vk1_s[h] = jnp.concatenate([values[:, part], keys[:, part], ones], axis=1)
        cq_s[h] = jnp.concatenate([cand[:, part], query[:, part]], axis=1)
    dvk_s[...] = jnp.zeros_like(dvk_s)
    first = lax.broadcasted_iota(jnp.int32, (BLOCK, 128), 1) < HEAD
    scale = 1.0 / (math.sqrt(HEAD) * math.log(2.0))

    def step(jb, carry):
        here = pl.ds(pl.multiple_of(jb * BLOCK, BLOCK), BLOCK)
        logit = jnp.zeros((BLOCK, 128), jnp.float32)
        kept = []
        for h in range(HEADS):
            part = slice(h * HEAD, (h + 1) * HEAD)
            cq = cq_s[h, here, :]
            score = dot(cq[:, HEAD:], kt_s[part, :])
            worth = dot(cq[:, :HEAD], vt_s[part, :])
            top = jnp.max(score, axis=1, keepdims=True)
            raised = jnp.exp2((score - top) * scale)
            ee_s[h, :BLOCK, :] = raised.astype(half)
            ee_s[h, BLOCK:, :] = (raised * worth).astype(half)
            both = dot(ee_s[h], vk1_s[h])
            inverse = 1.0 / both[:BLOCK, 128:]
            mean = both[BLOCK:, 128:] * inverse
            plain = both[:BLOCK, :128] * inverse
            lifted = both[BLOCK:, :128] * inverse - mean * plain
            logit = logit + mean
            kept.append((inverse, mean, plain, lifted))
        logit = logit / math.sqrt(WIDTH)
        factor = (GRAD_SCALE / math.sqrt(WIDTH)) * (jax.nn.sigmoid(logit) - jax.nn.sigmoid(teacher_ref[here, :]))
        direct, turned = [], []
        for h in range(HEADS):
            inverse, mean, plain, lifted = kept[h]
            cq = cq_s[h, here, :].astype(jnp.float32)
            weight = factor * inverse
            eighth = weight * (1.0 / math.sqrt(HEAD))
            xx_s[h, :BLOCK, :] = (cq * jnp.where(first, weight, -mean * eighth)).astype(half)
            xx_s[h, BLOCK:, :] = (cq * jnp.where(first, 0.0, eighth)).astype(half)
            dvk_s[h] += dot_tn(xx_s[h], ee_s[h])
            direct.append(plain[:, :HEAD] * factor[:, :HEAD])
            turned.append((lifted[:, HEAD:] * (factor[:, HEAD:] * (1.0 / math.sqrt(HEAD)))))
        back = jnp.concatenate(turned, axis=1).astype(half)
        grad = jnp.concatenate(direct, axis=1) + dot_nt(back, wq_ref[...])
        out_ref[here, :] = grad.astype(half)
        return carry

    lax.fori_loop(0, CAND // BLOCK, step, 0)
    dv = jnp.concatenate([dvk_s[h, :HEAD, :] for h in range(HEADS)], axis=0).astype(half)
    dk = jnp.concatenate([dvk_s[h, HEAD:, :] for h in range(HEADS)], axis=0).astype(half)
    grad_hist = dot_nt(dv.T, wv_ref[...]) + dot_nt(dk.T, wk_ref[...])
    out_ref[CAND:, :] = jnp.where(live2, grad_hist, 0.0).astype(half)


def attention(rows, length, teacher, w_query, w_key, w_value):
    half = jnp.bfloat16
    space = pl.BlockSpec(memory_space=pltpu.VMEM)
    return pl.pallas_call(
        attention_kernel,
        out_shape=jax.ShapeDtypeStruct((CAND + HIST, WIDTH), half),
        in_specs=[pl.BlockSpec(memory_space=pltpu.SMEM)] + [space] * 5,
        out_specs=space,
        scratch_shapes=[
            pltpu.VMEM((CAND, WIDTH), half),
            pltpu.VMEM((WIDTH, HIST), half),
            pltpu.VMEM((WIDTH, HIST), half),
            pltpu.VMEM((HEADS, HIST, 256), half),
            pltpu.VMEM((HEADS, CAND, 128), half),
            pltpu.VMEM((HEADS, 2 * BLOCK, HIST), half),
            pltpu.VMEM((HEADS, 2 * BLOCK, 128), half),
            pltpu.VMEM((HEADS, 128, HIST), jnp.float32),
        ],
        compiler_params=pltpu.CompilerParams(vmem_limit_bytes=48 * 2**20),
        cost_estimate=pl.CostEstimate(flops=4 * 10**9, bytes_accessed=3 * 2**20, transcendentals=4 * 2**20),
        name="attention",
    )(length, rows, jnp.broadcast_to(teacher.reshape(CAND, 1), (CAND, 128)), w_query, w_key, w_value)


USERS = 16
ITEMS = 8
PEERS = USERS * ITEMS
CAP = 40
TABLE_ROWS = 4096
GROUP = 8
SLOTS = GROUP * CAP
GROUPS = PEERS // GROUP
ROWS = CAND + HIST
MESH = pl.DeviceIdType.MESH


def partner(k, sign):
    dz = k % 4
    dx = (k // 4 + dz) % 4
    dy = (k // 16 + dz) % 4
    dc = k // 64
    user = lax.axis_index("user")
    item = lax.axis_index("item")
    z = (user // 4 + 4 + sign * dz) % 4
    x = (user % 4 + 4 + sign * dx) % 4
    y = (item // 2 + 4 + sign * dy) % 4
    c = (item % 2 + dc) % 2
    return z * 4 + x, y * 2 + c


def linear(where):
    return where[0] * ITEMS + where[1]


def one_hot(match):
    return jnp.where(match, 1.0, 0.0).astype(jnp.bfloat16)


def greet():
    user = lax.axis_index("user")
    item = lax.axis_index("item")
    barrier = pltpu.get_barrier_semaphore()
    for step in range(1, ITEMS):
        pl.semaphore_signal(barrier, inc=1, device_id=(user, (item + step) % ITEMS), device_id_type=MESH)
    for step in range(1, USERS):
        pl.semaphore_signal(barrier, inc=1, device_id=((user + step) % USERS, item), device_id_type=MESH)
    return barrier


def requests(cand_ref, hist_ref, place_ref):
    half = jnp.bfloat16
    rows = lax.broadcasted_iota(jnp.int32, (PEERS, 256), 0)
    slot = lax.broadcasted_iota(jnp.int32, (64, 256), 0).astype(jnp.float32)
    upper = one_hot(lax.broadcasted_iota(jnp.int32, (256, 256), 0) < lax.broadcasted_iota(jnp.int32, (256, 256), 1))
    taken = jnp.zeros((PEERS, 1), jnp.float32)
    wanted = jnp.zeros((PEERS, 128), jnp.float32)
    for c in range(ROWS // 256):
        at = c * 256
        ids = cand_ref[:, at:at + 256] if at < CAND else hist_ref[:, at - CAND:at - CAND + 256]
        owner = ids // TABLE_ROWS
        local = ids % TABLE_ROWS
        full = jnp.where(rows == owner, 1.0, 0.0)
        chosen = full.astype(half)
        rank = jnp.sum(full * (dot(chosen, upper) + taken), axis=0, keepdims=True)
        taken = taken + jnp.sum(full, axis=1, keepdims=True)
        place_ref[:, at:at + 256] = owner.astype(jnp.float32) * CAP + rank
        mine = slot == rank
        high = (local // 64).astype(jnp.float32)
        low = (local % 64).astype(jnp.float32)
        split = jnp.concatenate([jnp.where(mine, high, 0.0), jnp.where(mine, low, 0.0)], axis=0).astype(half)
        wanted = wanted + dot_nt(chosen, split)
    return jnp.concatenate([wanted[:, :64] * 64.0 + wanted[:, 64:], jnp.zeros((PEERS, 64), jnp.float32)], axis=1)


def fetch_kernel(cand_ref, hist_ref, table_ref, rows_ref, place_ref, asked_ref, want_s, item_out, item_in, user_out, wide_s, send_s, recv_s, pos_s, acc_s, isend, irecv, usend, urecv, rsend, rrecv):
    half = jnp.bfloat16
    user = lax.axis_index("user")
    item = lax.axis_index("item")
    barrier = greet()
    want_s[...] = requests(cand_ref, hist_ref, place_ref)
    for i in range(ITEMS):
        item_out[i] = want_s[pl.ds(i, USERS, stride=ITEMS), :]
    pl.semaphore_wait(barrier, USERS + ITEMS - 2)
    for step in range(1, ITEMS):
        to = (item + step) % ITEMS
        pltpu.make_async_remote_copy(
            src_ref=item_out.at[to], dst_ref=item_in.at[item], send_sem=isend, recv_sem=irecv,
            device_id=(user, to), device_id_type=MESH).start()
    item_in[item] = item_out[item]
    pos_s[...] = jnp.broadcast_to(place_ref[...], (128, ROWS)).T
    acc_s[...] = jnp.zeros_like(acc_s)
    pltpu.make_async_copy(item_out.at[pl.ds(1, ITEMS - 1)], item_in.at[pl.ds(1, ITEMS - 1)], irecv).wait()
    for u in range(USERS):
        user_out[u] = jnp.concatenate([item_in[i, u:u + 1, :] for i in range(ITEMS)], axis=0)
    for step in range(1, USERS):
        to = (user + step) % USERS
        pltpu.make_async_remote_copy(
            src_ref=user_out.at[to], dst_ref=asked_ref.at[user], send_sem=usend, recv_sem=urecv,
            device_id=(to, item), device_id_type=MESH).start()
    asked_ref[user] = user_out[user]
    pltpu.make_async_copy(user_out.at[pl.ds(1, USERS - 1)], asked_ref.at[pl.ds(1, USERS - 1)], urecv).wait()
    turned = asked_ref[...].reshape(PEERS, 128).T
    for p in range(PEERS):
        wide_s[p] = jnp.broadcast_to(turned[:CAP, p:p + 1], (CAP, 128))
    lane = lax.broadcasted_iota(jnp.int32, (SLOTS, 256), 1).astype(jnp.float32)

    def give(n, carry):
        wide = jnp.concatenate([wide_s[linear(partner(n * GROUP + kk, 1))] for kk in range(GROUP)], axis=0)
        ids = jnp.concatenate([wide, wide], axis=1)
        found = jnp.zeros((SLOTS, WIDTH), jnp.float32)
        for c in range(TABLE_ROWS // 256):
            found = found + dot(one_hot(ids == lane + c * 256.0), table_ref[c * 256:(c + 1) * 256, :])
        for kk in range(GROUP):
            k = n * GROUP + kk
            send_s[k] = found[kk * CAP:(kk + 1) * CAP].astype(half)

            def start():
                pltpu.make_async_remote_copy(
                    src_ref=send_s.at[k], dst_ref=recv_s.at[k], send_sem=rsend, recv_sem=rrecv.at[n],
                    device_id=partner(k, 1), device_id_type=MESH).start()

            if kk == 0:
                pl.when(n > 0)(start)
            else:
                start()
        return carry

    lax.fori_loop(0, GROUPS, give, 0)
    recv_s[0] = send_s[0]
    spot = lax.broadcasted_iota(jnp.int32, (8, SLOTS), 1)

    def take(n, carry):
        @pl.when(n == 0)
        def _():
            pltpu.make_async_copy(send_s.at[pl.ds(1, GROUP - 1)], recv_s.at[pl.ds(1, GROUP - 1)], rrecv.at[0]).wait()

        @pl.when(n > 0)
        def _():
            here = pl.ds(n * GROUP, GROUP)
            pltpu.make_async_copy(send_s.at[here], recv_s.at[here], rrecv.at[n]).wait()

        slab = recv_s[pl.ds(n * GROUP, GROUP)].astype(jnp.float32).reshape(SLOTS, WIDTH).astype(half)
        slots = jnp.zeros((8, SLOTS), jnp.int32)
        for kk in range(GROUP):
            base = (linear(partner(n * GROUP + kk, -1)) - kk) * CAP
            slots = jnp.where(spot >= kk * CAP, spot + base, slots)
        slots = slots[:1].astype(jnp.float32)
        for r in range(ROWS // 512):
            at = slice(r * 512, (r + 1) * 512)
            pos = pos_s[at, :]
            pos = jnp.concatenate([pos, pos, pos[:, :SLOTS - 256]], axis=1)
            acc_s[at, :] += dot(one_hot(pos == slots), slab)
        return carry

    lax.fori_loop(0, GROUPS, take, 0)
    rows_ref[...] = acc_s[...].astype(half)
    pltpu.make_async_copy(item_out.at[pl.ds(1, ITEMS - 1)], item_in.at[pl.ds(1, ITEMS - 1)], isend).wait()
    pltpu.make_async_copy(user_out.at[pl.ds(1, USERS - 1)], asked_ref.at[pl.ds(1, USERS - 1)], usend).wait()
    pltpu.make_async_copy(send_s.at[pl.ds(1, PEERS - 1)], recv_s.at[pl.ds(1, PEERS - 1)], rsend).wait()


def fetch(cand_ids, hist_ids, table):
    half = jnp.bfloat16
    space = pl.BlockSpec(memory_space=pltpu.VMEM)
    sem = pltpu.SemaphoreType.DMA
    return pl.pallas_call(
        fetch_kernel,
        out_shape=[
            jax.ShapeDtypeStruct((ROWS, WIDTH), half),
            jax.ShapeDtypeStruct((1, ROWS), jnp.float32),
            jax.ShapeDtypeStruct((USERS, ITEMS, 128), jnp.float32),
        ],
        in_specs=[space] * 3,
        out_specs=[space] * 3,
        scratch_shapes=[
            pltpu.VMEM((PEERS, 128), jnp.float32),
            pltpu.VMEM((ITEMS, USERS, 128), jnp.float32),
            pltpu.VMEM((ITEMS, USERS, 128), jnp.float32),
            pltpu.VMEM((USERS, ITEMS, 128), jnp.float32),
            pltpu.VMEM((PEERS, CAP, 128), jnp.float32),
            pltpu.VMEM((PEERS, CAP, WIDTH), half),
            pltpu.VMEM((PEERS, CAP, WIDTH), half),
            pltpu.VMEM((ROWS, 128), jnp.float32),
            pltpu.VMEM((ROWS, WIDTH), jnp.float32),
            sem(()), sem(()), sem(()), sem(()), sem(()), sem((GROUPS,)),
        ],
        compiler_params=pltpu.CompilerParams(collective_id=0, has_side_effects=True, vmem_limit_bytes=48 * 2**20),
        name="fetch",
    )(cand_ids, hist_ids, table)


def give_back_kernel(grad_ref, place_ref, asked_ref, out_ref, send_s, recv_s, known, rsend, rrecv):
    half = jnp.bfloat16
    user = lax.axis_index("user")
    item = lax.axis_index("item")
    barrier = greet()
    pl.semaphore_wait(barrier, USERS + ITEMS - 2)
    for step in range(1, USERS):
        pl.semaphore_signal(known, inc=1, device_id=((user + step) % USERS, item), device_id_type=MESH)
    pl.semaphore_wait(known, USERS - 1)
    deep = lax.broadcasted_iota(jnp.int32, (CAP, 128), 0)

    def give(n, carry):
        slots = jnp.concatenate([deep + linear(partner(n * GROUP + kk, 1)) * CAP for kk in range(GROUP)], axis=0)
        slots = slots.astype(jnp.float32)
        slots = jnp.concatenate([slots, slots], axis=1)
        found = jnp.zeros((SLOTS, WIDTH), jnp.float32)
        for c in range(ROWS // 256):
            at = slice(c * 256, (c + 1) * 256)
            found = found + dot(one_hot(slots == place_ref[:, at]), grad_ref[at, :])
        for kk in range(GROUP):
            k = n * GROUP + kk
            send_s[k] = found[kk * CAP:(kk + 1) * CAP].astype(half)

            def start():
                pltpu.make_async_remote_copy(
                    src_ref=send_s.at[k], dst_ref=recv_s.at[k], send_sem=rsend, recv_sem=rrecv.at[n],
                    device_id=partner(k, 1), device_id_type=MESH).start()

            if kk == 0:
                pl.when(n > 0)(start)
            else:
                start()
        return carry

    lax.fori_loop(0, GROUPS, give, 0)
    recv_s[0] = send_s[0]
    out_ref[...] = jnp.zeros_like(out_ref)
    high = lax.broadcasted_iota(jnp.int32, (512, SLOTS), 0).astype(jnp.float32)

    def take(n, carry):
        @pl.when(n == 0)
        def _():
            pltpu.make_async_copy(send_s.at[pl.ds(1, GROUP - 1)], recv_s.at[pl.ds(1, GROUP - 1)], rrecv.at[0]).wait()

        @pl.when(n > 0)
        def _():
            here = pl.ds(n * GROUP, GROUP)
            pltpu.make_async_copy(send_s.at[here], recv_s.at[here], rrecv.at[n]).wait()

        slab = recv_s[pl.ds(n * GROUP, GROUP)].astype(jnp.float32).reshape(SLOTS, WIDTH).astype(half)
        ids = []
        for kk in range(GROUP):
            source = partner(n * GROUP + kk, -1)
            ids.append(asked_ref[source[0], pl.ds(source[1], 1), :][:, :CAP])
        ids = jnp.concatenate(ids, axis=1)
        for r in range(TABLE_ROWS // 512):
            at = slice(r * 512, (r + 1) * 512)
            out_ref[at, :] += dot(one_hot(high + r * 512.0 == ids), slab)
        return carry

    lax.fori_loop(0, GROUPS, take, 0)
    pltpu.make_async_copy(send_s.at[pl.ds(1, PEERS - 1)], recv_s.at[pl.ds(1, PEERS - 1)], rsend).wait()


def give_back(grads, place, asked):
    half = jnp.bfloat16
    space = pl.BlockSpec(memory_space=pltpu.VMEM)
    sem = pltpu.SemaphoreType.DMA
    return pl.pallas_call(
        give_back_kernel,
        out_shape=jax.ShapeDtypeStruct((TABLE_ROWS, WIDTH), jnp.float32),
        in_specs=[space] * 3,
        out_specs=space,
        scratch_shapes=[
            pltpu.VMEM((PEERS, CAP, WIDTH), half),
            pltpu.VMEM((PEERS, CAP, WIDTH), half),
            pltpu.SemaphoreType.REGULAR,
            sem(()), sem((GROUPS,)),
        ],
        compiler_params=pltpu.CompilerParams(collective_id=1, has_side_effects=True, vmem_limit_bytes=48 * 2**20),
        name="give_back",
    )(grads, place, asked)


def body(cand_ids, hist_ids, hist_len, teacher, table, w_query, w_key, w_value):
    rows, place, asked = fetch(cand_ids, hist_ids, table)
    grads = attention(rows, hist_len, teacher, w_query, w_key, w_value)
    return give_back(grads, place, asked)


def solution(mesh):
    placed = (
        P(("user", "item"), None),
        P(("user", "item"), None),
        P(("user", "item")),
        P(("user", "item"), None),
        P(("user", "item"), None),
        P(),
        P(),
        P(),
    )
    return jax.shard_map(
        body, mesh=mesh, in_specs=placed, out_specs=P(("user", "item"), None), check_vma=False
    )
```

```python
import math

import jax
import jax.numpy as jnp
from jax import lax
from jax.experimental import pallas as pl
from jax.experimental.pallas import tpu as pltpu
from jax.sharding import PartitionSpec as P

HEADS = 4
GRAD_SCALE = 1024


CAND = 1024
HIST = 1024
WIDTH = 256
HEAD = 64
BLOCK = 256


def dot(a, b):
    return jnp.dot(a, b, preferred_element_type=jnp.float32)


def dot_tn(a, b):
    return lax.dot_general(a, b, (((0,), (0,)), ((), ())), preferred_element_type=jnp.float32)


def dot_nt(a, b):
    return lax.dot_general(a, b, (((1,), (1,)), ((), ())), preferred_element_type=jnp.float32)


def attend(length, rows_ref, teacher_ref, wq_ref, wk_ref, wv_ref, out_ref, kt_s, vt_s, vk1_s, cq_s, ee_s, xx_s, dvk_s):
    half = jnp.bfloat16
    live = lax.broadcasted_iota(jnp.int32, (HIST, 128), 0) < length
    live2 = jnp.concatenate([live, live], axis=1)
    hist = jnp.where(live2, rows_ref[CAND:, :], jnp.zeros((), half))
    keys = dot(hist, wk_ref[...]).astype(half)
    values = dot(hist, wv_ref[...]).astype(half)
    kt_s[...] = keys.T
    vt_s[...] = values.T
    cand = rows_ref[:CAND, :]
    query = dot(cand, wq_ref[...]).astype(half)
    ones = jnp.where(live, 1.0, 0.0).astype(half)
    for h in range(HEADS):
        part = slice(h * HEAD, (h + 1) * HEAD)
        vk1_s[h] = jnp.concatenate([values[:, part], keys[:, part], ones], axis=1)
        cq_s[h] = jnp.concatenate([cand[:, part], query[:, part]], axis=1)
    dvk_s[...] = jnp.zeros_like(dvk_s)
    first = lax.broadcasted_iota(jnp.int32, (BLOCK, 128), 1) < HEAD
    scale = 1.0 / (math.sqrt(HEAD) * math.log(2.0))

    def step(jb, carry):
        here = pl.ds(pl.multiple_of(jb * BLOCK, BLOCK), BLOCK)
        logit = jnp.zeros((BLOCK, 128), jnp.float32)
        kept = []
        for h in range(HEADS):
            part = slice(h * HEAD, (h + 1) * HEAD)
            cq = cq_s[h, here, :]
            score = dot(cq[:, HEAD:], kt_s[part, :])
            worth = dot(cq[:, :HEAD], vt_s[part, :])
            top = jnp.max(score, axis=1, keepdims=True)
            raised = jnp.exp2((score - top) * scale)
            ee_s[h, :BLOCK, :] = raised.astype(half)
            ee_s[h, BLOCK:, :] = (raised * worth).astype(half)
            both = dot(ee_s[h], vk1_s[h])
            inverse = 1.0 / both[:BLOCK, 128:]
            mean = both[BLOCK:, 128:] * inverse
            plain = both[:BLOCK, :128] * inverse
            lifted = both[BLOCK:, :128] * inverse - mean * plain
            logit = logit + mean
            kept.append((inverse, mean, plain, lifted))
        logit = logit / math.sqrt(WIDTH)
        factor = (GRAD_SCALE / math.sqrt(WIDTH)) * (jax.nn.sigmoid(logit) - jax.nn.sigmoid(teacher_ref[here, :]))
        direct, turned = [], []
        for h in range(HEADS):
            inverse, mean, plain, lifted = kept[h]
            cq = cq_s[h, here, :].astype(jnp.float32)
            weight = factor * inverse
            eighth = weight * (1.0 / math.sqrt(HEAD))
            xx_s[h, :BLOCK, :] = (cq * jnp.where(first, weight, -mean * eighth)).astype(half)
            xx_s[h, BLOCK:, :] = (cq * jnp.where(first, 0.0, eighth)).astype(half)
            dvk_s[h] += dot_tn(xx_s[h], ee_s[h])
            direct.append(plain[:, :HEAD] * factor[:, :HEAD])
            turned.append((lifted[:, HEAD:] * (factor[:, HEAD:] * (1.0 / math.sqrt(HEAD)))))
        back = jnp.concatenate(turned, axis=1).astype(half)
        grad = jnp.concatenate(direct, axis=1) + dot_nt(back, wq_ref[...])
        out_ref[here, :] = grad.astype(half)
        return carry

    lax.fori_loop(0, CAND // BLOCK, step, 0)
    dv = jnp.concatenate([dvk_s[h, :HEAD, :] for h in range(HEADS)], axis=0).astype(half)
    dk = jnp.concatenate([dvk_s[h, HEAD:, :] for h in range(HEADS)], axis=0).astype(half)
    grad_hist = dot_nt(dv.T, wv_ref[...]) + dot_nt(dk.T, wk_ref[...])
    out_ref[CAND:, :] = jnp.where(live2, grad_hist, 0.0).astype(half)


USERS = 16
ITEMS = 8
PEERS = USERS * ITEMS
CAP = 40
TABLE_ROWS = 4096
ROWS = CAND + HIST
SUB = 6
PART = SUB * CAP
PAIR = 2 * SUB
STEPS = 11
PADDED = STEPS * PAIR
LAG = 5
LEAD = 11
MESH = pl.DeviceIdType.MESH


def partner(k, sign):
    dz = k % 4
    dx = (k // 4 + dz) % 4
    dy = (k // 16 + dz) % 4
    dc = k // 64
    user = lax.axis_index("user")
    item = lax.axis_index("item")
    z = (user // 4 + 4 + sign * dz) % 4
    x = (user % 4 + 4 + sign * dx) % 4
    y = (item // 2 + 4 + sign * dy) % 4
    c = (item % 2 + dc) % 2
    return z * 4 + x, y * 2 + c


def partner_index(owner):
    user = lax.axis_index("user")
    item = lax.axis_index("item")
    dz = (user // 4 - owner // 32) & 3
    a = (user % 4 - owner // 8 - dz) & 3
    b = (item // 2 - owner // 2 - dz) & 3
    dc = (item - owner) & 1
    return dc * 64 + b * 16 + a * 4 + dz


def linear(where):
    return where[0] * ITEMS + where[1]


def one_hot(match):
    return jnp.where(match, 1.0, 0.0).astype(jnp.bfloat16)


def keep(match, value):
    return jnp.where(match, value, jnp.zeros((), value.dtype))


def greet():
    user = lax.axis_index("user")
    item = lax.axis_index("item")
    barrier = pltpu.get_barrier_semaphore()
    for step in range(1, ITEMS):
        pl.semaphore_signal(barrier, inc=1, device_id=(user, (item + step) % ITEMS), device_id_type=MESH)
    for step in range(1, USERS):
        pl.semaphore_signal(barrier, inc=1, device_id=((user + step) % USERS, item), device_id_type=MESH)
    return barrier


def requests(cand_ref, hist_ref, high_ref, low_ref):
    half = jnp.bfloat16
    rows = lax.broadcasted_iota(jnp.int32, (PEERS, 256), 0)
    slot = lax.broadcasted_iota(jnp.int32, (64, 256), 0).astype(jnp.float32)
    upper = one_hot(lax.broadcasted_iota(jnp.int32, (256, 256), 0) < lax.broadcasted_iota(jnp.int32, (256, 256), 1))
    taken = jnp.zeros((PEERS, 1), jnp.float32)
    wanted = jnp.zeros((PEERS, 128), jnp.float32)
    for c in range(ROWS // 256):
        at = c * 256
        ids = cand_ref[:, at:at + 256] if at < CAND else hist_ref[:, at - CAND:at - CAND + 256]
        owner = ids // TABLE_ROWS
        local = ids % TABLE_ROWS
        full = jnp.where(rows == owner, 1.0, 0.0)
        chosen = full.astype(half)
        rank = jnp.sum(full * (dot(chosen, upper) + taken), axis=0, keepdims=True)
        taken = taken + jnp.sum(full, axis=1, keepdims=True)
        k = partner_index(owner)
        part = (k * 43) // 256
        high_ref[:, at:at + 256] = part.astype(jnp.float32)
        low_ref[:, at:at + 256] = ((k - part * SUB) * CAP).astype(jnp.float32) + rank
        mine = slot == rank
        upper_half = (local // 64).astype(jnp.float32)
        lower_half = (local % 64).astype(jnp.float32)
        split = jnp.concatenate([jnp.where(mine, upper_half, 0.0), jnp.where(mine, lower_half, 0.0)], axis=0).astype(half)
        wanted = wanted + dot_nt(chosen, split)
    return jnp.concatenate([wanted[:, :64] * 64.0 + wanted[:, 64:], jnp.zeros((PEERS, 64), jnp.float32)], axis=1)


def send_part(n, found, buffer, landing, send_sem, recv_sem, sign):
    for kk in range(PAIR):
        k = n * PAIR + kk
        buffer[k] = found[kk * CAP:(kk + 1) * CAP].astype(jnp.bfloat16)

        def start():
            pltpu.make_async_remote_copy(
                src_ref=buffer.at[k], dst_ref=landing.at[k], send_sem=send_sem, recv_sem=recv_sem.at[n],
                device_id=partner(k, sign), device_id_type=MESH).start()

        if kk == 0:
            pl.when(n > 0)(start)
        elif kk < PEERS - (STEPS - 1) * PAIR:
            start()
        else:
            pl.when(n < STEPS - 1)(start)


def landed(n, buffer, landing, recv_sem):
    def wait(first, count):
        here = pl.ds(first, count)
        pltpu.make_async_copy(buffer.at[here], landing.at[here], recv_sem.at[n]).wait()

    @pl.when(n == 0)
    def _():
        wait(1, PAIR - 1)

    @pl.when(jnp.logical_and(n > 0, n < STEPS - 1))
    def _():
        wait(n * PAIR, PAIR)

    @pl.when(n == STEPS - 1)
    def _():
        wait((STEPS - 1) * PAIR, PEERS - (STEPS - 1) * PAIR)


def slabs(n, landing):
    half = jnp.bfloat16
    tail = jnp.zeros((256 - PART, WIDTH), half)
    parts = []
    for s in range(2):
        part = landing[pl.ds(n * PAIR + s * SUB, SUB)].astype(jnp.float32).reshape(PART, WIDTH).astype(half)
        parts += [part, tail]
    return jnp.concatenate(parts, axis=0)


def number(value, shape):
    return jnp.broadcast_to(jnp.asarray(value, jnp.int32).astype(jnp.float32), shape).astype(jnp.bfloat16)


def ranker_kernel(
    len_ref, cand_ref, hist_ref, teacher_ref, table_any, wq_any, wk_any, wv_any, out_ref,
    table_ref, wq_ref, wk_ref, wv_ref, high_ref, low_ref, want_s, item_out, item_in, user_out, asked_ref, wide_s,
    send_s, recv_s, back_s, home_s, low_col, high_col, low_row, acc_s, rows_ref, grad_ref, aim_s,
    kt_s, vt_s, vk1_s, cq_s, ee_s, xx_s, dvk_s,
    local, isend, irecv, usend, urecv, rsend, rrecv, gsend, grecv,
):
    half = jnp.bfloat16
    full = jnp.float32
    user = lax.axis_index("user")
    item = lax.axis_index("item")
    barrier = greet()
    loads = [
        pltpu.make_async_copy(src, dst, local.at[n])
        for n, (src, dst) in enumerate([(table_any, table_ref), (wq_any, wq_ref), (wk_any, wk_ref), (wv_any, wv_ref)])
    ]
    for load in loads:
        load.start()
    want_s[...] = requests(cand_ref, hist_ref, high_ref, low_ref)
    for i in range(ITEMS):
        item_out[i] = want_s[pl.ds(i, USERS, stride=ITEMS), :]
    pl.semaphore_wait(barrier, USERS + ITEMS - 2)
    for step in range(1, ITEMS):
        to = (item + step) % ITEMS
        pltpu.make_async_remote_copy(
            src_ref=item_out.at[to], dst_ref=item_in.at[item], send_sem=isend, recv_sem=irecv,
            device_id=(user, to), device_id_type=MESH).start()
    item_in[item] = item_out[item]
    low = jnp.broadcast_to(low_ref[...], (128, ROWS)).T
    lane = lax.broadcasted_iota(jnp.int32, (ROWS, 128), 1).astype(full)
    low_col[:, :128] = one_hot(low == lane)
    low_col[:, 128:] = one_hot(low == lane + 128.0)
    high_col[...] = jnp.broadcast_to(high_ref[...], (128, ROWS)).T.astype(half)
    low_row[...] = one_hot(low_ref[...] == lax.broadcasted_iota(jnp.int32, (PART, ROWS), 0).astype(full))
    pltpu.make_async_copy(item_out.at[pl.ds(1, ITEMS - 1)], item_in.at[pl.ds(1, ITEMS - 1)], irecv).wait()
    for u in range(USERS):
        user_out[u] = jnp.concatenate([item_in[i, u:u + 1, :] for i in range(ITEMS)], axis=0)
    for step in range(1, USERS):
        to = (user + step) % USERS
        pltpu.make_async_remote_copy(
            src_ref=user_out.at[to], dst_ref=asked_ref.at[user], send_sem=usend, recv_sem=urecv,
            device_id=(to, item), device_id_type=MESH).start()
    asked_ref[user] = user_out[user]
    acc_s[...] = jnp.zeros_like(acc_s)
    aim_s[...] = jnp.broadcast_to(teacher_ref[...], (128, CAND)).T
    out_ref[...] = jnp.zeros_like(out_ref)
    for spare in range(PEERS, PADDED):
        recv_s[spare] = jnp.zeros((CAP, WIDTH), half)
        home_s[spare] = jnp.zeros((CAP, WIDTH), half)
    pltpu.make_async_copy(user_out.at[pl.ds(1, USERS - 1)], asked_ref.at[pl.ds(1, USERS - 1)], urecv).wait()
    loads[0].wait()
    turned = asked_ref[...].reshape(PEERS, 128).T
    for p in range(PEERS):
        wide_s[p] = jnp.broadcast_to(turned[:CAP, p:p + 1], (CAP, 128))
    lane = lax.broadcasted_iota(jnp.int32, (2 * PART, 128), 1).astype(full)

    def give(n, carry):
        ids = jnp.concatenate([wide_s[linear(partner(n * PAIR + kk, 1))] for kk in range(PAIR)], axis=0)
        high = jnp.floor(ids * (1.0 / 256.0))
        low = ids - high * 256.0
        low = jnp.concatenate([one_hot(low == lane), one_hot(low == lane + 128.0)], axis=1)
        high = high.astype(half)
        high = jnp.concatenate([high, high], axis=1)
        found = jnp.zeros((2 * PART, WIDTH), full)
        for c in range(TABLE_ROWS // 256):
            found = found + dot(keep(high == number(c, (1, 1)), low), table_ref[c * 256:(c + 1) * 256, :])
        send_part(n, found, send_s, recv_s, rsend, rrecv, 1)
        return carry

    def take(n, carry):
        landed(n, send_s, recv_s, rrecv)
        slab = slabs(n, recv_s)
        for r in range(ROWS // 512):
            at = slice(r * 512, (r + 1) * 512)
            high = high_col[at, :]
            high = jnp.concatenate([high, high], axis=1)
            low = low_col[at, :]
            picked = jnp.concatenate([keep(high == number(2 * n + s, (1, 256)), low) for s in range(2)], axis=1)
            acc_s[at, :] += dot(picked, slab)
        return carry

    lax.fori_loop(0, LEAD, give, 0)
    recv_s[0] = send_s[0]
    lax.fori_loop(LEAD, STEPS, lambda n, carry: take(n - LEAD, give(n, carry)), 0)
    lax.fori_loop(STEPS - LEAD, STEPS, take, 0)
    rows_ref[...] = acc_s[...].astype(half)
    for load in loads[1:]:
        load.wait()
    attend(len_ref[0], rows_ref, aim_s, wq_ref, wk_ref, wv_ref, grad_ref, kt_s, vt_s, vk1_s, cq_s, ee_s, xx_s, dvk_s)
    high_row = jnp.broadcast_to(high_ref[...], (16, ROWS))

    def give_back(n, carry):
        found = []
        for s in range(2):
            match = one_hot(high_row == (2 * n + s).astype(full))
            part = jnp.zeros((PART, WIDTH), full)
            for c in range(ROWS // 512):
                at = slice(c * 512, (c + 1) * 512)
                mine = jnp.concatenate([match[:, at]] * (PART // 16), axis=0)
                part = part + dot(mine * low_row[:, at], grad_ref[at, :])
            found.append(part)
        send_part(n, jnp.concatenate(found, axis=0), back_s, home_s, gsend, grecv, -1)
        return carry

    deep = lax.broadcasted_iota(jnp.int32, (256, 512), 0).astype(full)

    def take_back(n, carry):
        landed(n, back_s, home_s, grecv)
        slab = slabs(n, home_s)
        ids = []
        for kk in range(PAIR):
            source = partner(n * PAIR + kk, 1)
            ids.append(asked_ref[source[0], pl.ds(source[1], 1), :][:, :CAP])
            if kk % SUB == SUB - 1:
                ids.append(jnp.zeros((1, 256 - PART), full))
        ids = jnp.concatenate(ids, axis=1)
        high = jnp.floor(ids * (1.0 / 256.0))
        low = one_hot(ids - high * 256.0 == deep)
        high = jnp.broadcast_to(high, (16, 512))
        for c in range(0, TABLE_ROWS // 256, 2):
            picked = []
            for d in range(2):
                mine = one_hot(high == float(c + d))
                picked.append(jnp.concatenate([mine] * 16, axis=0) * low)
            at = slice(c * 256, (c + 2) * 256)
            out_ref[at, :] += dot(jnp.concatenate(picked, axis=0), slab)
        return carry

    lax.fori_loop(0, LAG, give_back, 0)
    home_s[0] = back_s[0]
    lax.fori_loop(LAG, STEPS, lambda n, carry: take_back(n - LAG, give_back(n, carry)), 0)
    lax.fori_loop(STEPS - LAG, STEPS, take_back, 0)
    pltpu.make_async_copy(back_s.at[pl.ds(1, PEERS - 1)], home_s.at[pl.ds(1, PEERS - 1)], gsend).wait()
    pltpu.make_async_copy(item_out.at[pl.ds(1, ITEMS - 1)], item_in.at[pl.ds(1, ITEMS - 1)], isend).wait()
    pltpu.make_async_copy(user_out.at[pl.ds(1, USERS - 1)], asked_ref.at[pl.ds(1, USERS - 1)], usend).wait()
    pltpu.make_async_copy(send_s.at[pl.ds(1, PEERS - 1)], recv_s.at[pl.ds(1, PEERS - 1)], rsend).wait()


def body(cand_ids, hist_ids, hist_len, teacher, table, w_query, w_key, w_value):
    half = jnp.bfloat16
    full = jnp.float32
    space = pl.BlockSpec(memory_space=pltpu.VMEM)
    anywhere = pl.BlockSpec(memory_space=pltpu.HBM)
    sem = pltpu.SemaphoreType.DMA
    vmem = pltpu.VMEM
    return pl.pallas_call(
        ranker_kernel,
        out_shape=pltpu.VMEM((TABLE_ROWS, WIDTH), full),
        in_specs=[pl.BlockSpec(memory_space=pltpu.SMEM)] + [space] * 3 + [anywhere] * 4,
        out_specs=space,
        scratch_shapes=[
            vmem((TABLE_ROWS, WIDTH), half),
            vmem((WIDTH, WIDTH), half),
            vmem((WIDTH, WIDTH), half),
            vmem((WIDTH, WIDTH), half),
            vmem((1, ROWS), full),
            vmem((1, ROWS), full),
            vmem((PEERS, 128), full),
            vmem((ITEMS, USERS, 128), full),
            vmem((ITEMS, USERS, 128), full),
            vmem((USERS, ITEMS, 128), full),
            vmem((USERS, ITEMS, 128), full),
            vmem((PEERS, CAP, 128), full),
            vmem((PADDED, CAP, WIDTH), half),
            vmem((PADDED, CAP, WIDTH), half),
            vmem((PADDED, CAP, WIDTH), half),
            vmem((PADDED, CAP, WIDTH), half),
            vmem((ROWS, 256), half),
            vmem((ROWS, 128), half),
            vmem((PART, ROWS), half),
            vmem((ROWS, WIDTH), full),
            vmem((ROWS, WIDTH), half),
            vmem((ROWS, WIDTH), half),
            vmem((CAND, 128), full),
            vmem((WIDTH, HIST), half),
            vmem((WIDTH, HIST), half),
            vmem((HEADS, HIST, 256), half),
            vmem((HEADS, CAND, 128), half),
            vmem((HEADS, 2 * BLOCK, HIST), half),
            vmem((HEADS, 2 * BLOCK, 128), half),
            vmem((HEADS, 128, HIST), full),
            sem((4,)), sem(()), sem(()), sem(()), sem(()), sem(()), sem((STEPS,)), sem(()), sem((STEPS,)),
        ],
        compiler_params=pltpu.CompilerParams(collective_id=0, has_side_effects=True, vmem_limit_bytes=56 * 2**20),
        name="ranker",
    )(hist_len, cand_ids, hist_ids, teacher, *(pltpu.with_memory_space_constraint(x, pltpu.HBM) for x in (table, w_query, w_key, w_value)))


def solution(mesh):
    placed = (
        P(("user", "item"), None),
        P(("user", "item"), None),
        P(("user", "item")),
        P(("user", "item"), None),
        P(("user", "item"), None),
        P(),
        P(),
        P(),
    )
    return jax.shard_map(
        body, mesh=mesh, in_specs=placed, out_specs=P(("user", "item"), None), check_vma=False
    )
```

```python
import math

import jax
import jax.numpy as jnp
from jax import lax
from jax.experimental import pallas as pl
from jax.experimental.pallas import tpu as pltpu
from jax.sharding import PartitionSpec as P

HEADS = 4
GRAD_SCALE = 1024


CAND = 1024
HIST = 1024
WIDTH = 256
HEAD = 64
BLOCK = 512


def dot(a, b):
    return jnp.dot(a, b, preferred_element_type=jnp.float32)


def dot_tn(a, b):
    return lax.dot_general(a, b, (((0,), (0,)), ((), ())), preferred_element_type=jnp.float32)


def dot_nt(a, b):
    return lax.dot_general(a, b, (((1,), (1,)), ((), ())), preferred_element_type=jnp.float32)


def attend(length, rows_ref, teacher_ref, wq_ref, wk_ref, wv_ref, out_ref, kt_s, vt_s, vk1_s, cq_s, ee_s, xx_s, dvk_s):
    half = jnp.bfloat16
    live = lax.broadcasted_iota(jnp.int32, (HIST, 128), 0) < length
    live2 = jnp.concatenate([live, live], axis=1)
    hist = jnp.where(live2, rows_ref[CAND:, :], jnp.zeros((), half))
    keys = dot(hist, wk_ref[...]).astype(half)
    values = dot(hist, wv_ref[...]).astype(half)
    kt_s[...] = keys.T
    vt_s[...] = values.T
    cand = rows_ref[:CAND, :]
    query = dot(cand, wq_ref[...]).astype(half)
    ones = jnp.where(live, 1.0, 0.0).astype(half)
    for h in range(HEADS):
        part = slice(h * HEAD, (h + 1) * HEAD)
        vk1_s[h] = jnp.concatenate([values[:, part], keys[:, part], ones], axis=1)
        cq_s[h] = jnp.concatenate([cand[:, part], query[:, part]], axis=1)
    dvk_s[...] = jnp.zeros_like(dvk_s)
    first = lax.broadcasted_iota(jnp.int32, (BLOCK, 128), 1) < HEAD
    scale = 1.0 / (math.sqrt(HEAD) * math.log(2.0))

    def step(jb, carry):
        here = pl.ds(pl.multiple_of(jb * BLOCK, BLOCK), BLOCK)
        logit = jnp.zeros((BLOCK, 128), jnp.float32)
        kept = []
        for h in range(HEADS):
            part = slice(h * HEAD, (h + 1) * HEAD)
            cq = cq_s[h, here, :]
            score = dot(cq[:, HEAD:], kt_s[part, :])
            worth = dot(cq[:, :HEAD], vt_s[part, :])
            top = jnp.max(score, axis=1, keepdims=True)
            raised = jnp.exp2((score - top) * scale)
            ee_s[h, :BLOCK, :] = raised.astype(half)
            ee_s[h, BLOCK:, :] = (raised * worth).astype(half)
            both = dot(ee_s[h], vk1_s[h])
            inverse = 1.0 / both[:BLOCK, 128:]
            mean = both[BLOCK:, 128:] * inverse
            plain = both[:BLOCK, :128] * inverse
            lifted = both[BLOCK:, :128] * inverse - mean * plain
            logit = logit + mean
            kept.append((inverse, mean, plain, lifted))
        logit = logit / math.sqrt(WIDTH)
        factor = (GRAD_SCALE / math.sqrt(WIDTH)) * (jax.nn.sigmoid(logit) - jax.nn.sigmoid(teacher_ref[here, :]))
        direct, turned = [], []
        for h in range(HEADS):
            inverse, mean, plain, lifted = kept[h]
            cq = cq_s[h, here, :].astype(jnp.float32)
            weight = factor * inverse
            eighth = weight * (1.0 / math.sqrt(HEAD))
            xx_s[h, :BLOCK, :] = (cq * jnp.where(first, weight, -mean * eighth)).astype(half)
            xx_s[h, BLOCK:, :] = (cq * jnp.where(first, 0.0, eighth)).astype(half)
            dvk_s[h] += dot_tn(xx_s[h], ee_s[h])
            direct.append(plain[:, :HEAD] * factor[:, :HEAD])
            turned.append((lifted[:, HEAD:] * (factor[:, HEAD:] * (1.0 / math.sqrt(HEAD)))))
        back = jnp.concatenate(turned, axis=1).astype(half)
        grad = jnp.concatenate(direct, axis=1) + dot_nt(back, wq_ref[...])
        out_ref[here, :] = grad.astype(half)
        return carry

    lax.fori_loop(0, CAND // BLOCK, step, 0)
    dv = jnp.concatenate([dvk_s[h, :HEAD, :] for h in range(HEADS)], axis=0).astype(half)
    dk = jnp.concatenate([dvk_s[h, HEAD:, :] for h in range(HEADS)], axis=0).astype(half)
    grad_hist = dot_nt(dv.T, wv_ref[...]) + dot_nt(dk.T, wk_ref[...])
    out_ref[CAND:, :] = jnp.where(live2, grad_hist, 0.0).astype(half)


USERS = 16
ITEMS = 8
PEERS = USERS * ITEMS
CAP = 40
TABLE_ROWS = 4096
ROWS = CAND + HIST
SUB = 6
PART = SUB * CAP
PAIR = 2 * SUB
STEPS = 11
PADDED = STEPS * PAIR
LAG = 5
LEAD = 11
MESH = pl.DeviceIdType.MESH


def partner(k, sign):
    dz = k % 4
    dx = (k // 4 + dz) % 4
    dy = (k // 16 + dz) % 4
    dc = k // 64
    user = lax.axis_index("user")
    item = lax.axis_index("item")
    z = (user // 4 + 4 + sign * dz) % 4
    x = (user % 4 + 4 + sign * dx) % 4
    y = (item // 2 + 4 + sign * dy) % 4
    c = (item % 2 + dc) % 2
    return z * 4 + x, y * 2 + c


def partner_index(owner):
    user = lax.axis_index("user")
    item = lax.axis_index("item")
    dz = (user // 4 - owner // 32) & 3
    a = (user % 4 - owner // 8 - dz) & 3
    b = (item // 2 - owner // 2 - dz) & 3
    dc = (item - owner) & 1
    return dc * 64 + b * 16 + a * 4 + dz


def linear(where):
    return where[0] * ITEMS + where[1]


def one_hot(match):
    return jnp.where(match, 1.0, 0.0).astype(jnp.bfloat16)


def keep(match, value):
    return jnp.where(match, value, jnp.zeros((), value.dtype))


def greet():
    user = lax.axis_index("user")
    item = lax.axis_index("item")
    barrier = pltpu.get_barrier_semaphore()
    for step in range(1, ITEMS):
        pl.semaphore_signal(barrier, inc=1, device_id=(user, (item + step) % ITEMS), device_id_type=MESH)
    for step in range(1, USERS):
        pl.semaphore_signal(barrier, inc=1, device_id=((user + step) % USERS, item), device_id_type=MESH)
    return barrier


def requests(cand_ref, hist_ref, high_ref, low_ref):
    half = jnp.bfloat16
    rows = lax.broadcasted_iota(jnp.int32, (PEERS, 256), 0)
    slot = lax.broadcasted_iota(jnp.int32, (64, 256), 0).astype(jnp.float32)
    upper = one_hot(lax.broadcasted_iota(jnp.int32, (256, 256), 0) < lax.broadcasted_iota(jnp.int32, (256, 256), 1))
    taken = jnp.zeros((PEERS, 1), jnp.float32)
    wanted = jnp.zeros((PEERS, 128), jnp.float32)
    for c in range(ROWS // 256):
        at = c * 256
        ids = cand_ref[:, at:at + 256] if at < CAND else hist_ref[:, at - CAND:at - CAND + 256]
        owner = ids // TABLE_ROWS
        local = ids % TABLE_ROWS
        full = jnp.where(rows == owner, 1.0, 0.0)
        chosen = full.astype(half)
        rank = jnp.sum(full * (dot(chosen, upper) + taken), axis=0, keepdims=True)
        taken = taken + jnp.sum(full, axis=1, keepdims=True)
        k = partner_index(owner)
        part = (k * 43) // 256
        high_ref[:, at:at + 256] = part.astype(jnp.float32)
        low_ref[:, at:at + 256] = ((k - part * SUB) * CAP).astype(jnp.float32) + rank
        mine = slot == rank
        upper_half = (local // 64).astype(jnp.float32)
        lower_half = (local % 64).astype(jnp.float32)
        split = jnp.concatenate([jnp.where(mine, upper_half, 0.0), jnp.where(mine, lower_half, 0.0)], axis=0).astype(half)
        wanted = wanted + dot_nt(chosen, split)
    return jnp.concatenate([wanted[:, :64] * 64.0 + wanted[:, 64:], jnp.zeros((PEERS, 64), jnp.float32)], axis=1)


def send_part(n, found, buffer, landing, send_sem, recv_sem, sign):
    for kk in range(PAIR):
        k = n * PAIR + kk
        buffer[k] = found[kk * CAP:(kk + 1) * CAP].astype(jnp.bfloat16)

        def start():
            pltpu.make_async_remote_copy(
                src_ref=buffer.at[k], dst_ref=landing.at[k], send_sem=send_sem, recv_sem=recv_sem.at[n],
                device_id=partner(k, sign), device_id_type=MESH).start()

        if kk == 0:
            pl.when(n > 0)(start)
        elif kk < PEERS - (STEPS - 1) * PAIR:
            start()
        else:
            pl.when(n < STEPS - 1)(start)


def landed(n, buffer, landing, recv_sem):
    def wait(first, count):
        here = pl.ds(first, count)
        pltpu.make_async_copy(buffer.at[here], landing.at[here], recv_sem.at[n]).wait()

    @pl.when(n == 0)
    def _():
        wait(1, PAIR - 1)

    @pl.when(jnp.logical_and(n > 0, n < STEPS - 1))
    def _():
        wait(n * PAIR, PAIR)

    @pl.when(n == STEPS - 1)
    def _():
        wait((STEPS - 1) * PAIR, PEERS - (STEPS - 1) * PAIR)


def slabs(n, landing):
    half = jnp.bfloat16
    tail = jnp.zeros((256 - PART, WIDTH), half)
    parts = []
    for s in range(2):
        part = landing[pl.ds(n * PAIR + s * SUB, SUB)].astype(jnp.float32).reshape(PART, WIDTH).astype(half)
        parts += [part, tail]
    return jnp.concatenate(parts, axis=0)


def number(value, shape):
    return jnp.broadcast_to(jnp.asarray(value, jnp.int32).astype(jnp.float32), shape).astype(jnp.bfloat16)


def ranker_kernel(
    len_ref, cand_ref, hist_ref, teacher_ref, table_any, wq_any, wk_any, wv_any, out_ref,
    table_ref, wq_ref, wk_ref, wv_ref, high_ref, low_ref, want_s, item_out, item_in, user_out, asked_ref, wide_s,
    send_s, recv_s, back_s, home_s, low_col, high_col, low_row, acc_s, rows_ref, grad_ref, aim_s,
    kt_s, vt_s, vk1_s, cq_s, ee_s, xx_s, dvk_s,
    local, isend, irecv, usend, urecv, rsend, rrecv, gsend, grecv,
):
    half = jnp.bfloat16
    full = jnp.float32
    user = lax.axis_index("user")
    item = lax.axis_index("item")
    barrier = greet()
    loads = [
        pltpu.make_async_copy(src, dst, local.at[n])
        for n, (src, dst) in enumerate([(table_any, table_ref), (wq_any, wq_ref), (wk_any, wk_ref), (wv_any, wv_ref)])
    ]
    for load in loads:
        load.start()
    want_s[...] = requests(cand_ref, hist_ref, high_ref, low_ref)
    for i in range(ITEMS):
        item_out[i] = want_s[pl.ds(i, USERS, stride=ITEMS), :]
    pl.semaphore_wait(barrier, USERS + ITEMS - 2)
    for step in range(1, ITEMS):
        to = (item + step) % ITEMS
        pltpu.make_async_remote_copy(
            src_ref=item_out.at[to], dst_ref=item_in.at[item], send_sem=isend, recv_sem=irecv,
            device_id=(user, to), device_id_type=MESH).start()
    item_in[item] = item_out[item]
    pltpu.make_async_copy(item_out.at[pl.ds(1, ITEMS - 1)], item_in.at[pl.ds(1, ITEMS - 1)], irecv).wait()
    for u in range(USERS):
        user_out[u] = jnp.concatenate([item_in[i, u:u + 1, :] for i in range(ITEMS)], axis=0)
    for step in range(1, USERS):
        to = (user + step) % USERS
        pltpu.make_async_remote_copy(
            src_ref=user_out.at[to], dst_ref=asked_ref.at[user], send_sem=usend, recv_sem=urecv,
            device_id=(to, item), device_id_type=MESH).start()
    asked_ref[user] = user_out[user]
    pltpu.make_async_copy(user_out.at[pl.ds(1, USERS - 1)], asked_ref.at[pl.ds(1, USERS - 1)], urecv).wait()
    loads[0].wait()
    turned = asked_ref[...].reshape(PEERS, 128).T
    for p in range(PEERS):
        wide_s[p] = jnp.broadcast_to(turned[:CAP, p:p + 1], (CAP, 128))
    lane = lax.broadcasted_iota(jnp.int32, (2 * PART, 128), 1).astype(full)

    def give(n, carry):
        ids = jnp.concatenate([wide_s[linear(partner(n * PAIR + kk, 1))] for kk in range(PAIR)], axis=0)
        high = jnp.floor(ids * (1.0 / 256.0))
        low = ids - high * 256.0
        low = jnp.concatenate([one_hot(low == lane), one_hot(low == lane + 128.0)], axis=1)
        high = high.astype(half)
        high = jnp.concatenate([high, high], axis=1)
        found = jnp.zeros((2 * PART, WIDTH), full)
        for c in range(TABLE_ROWS // 256):
            found = found + dot(keep(high == number(c, (1, 1)), low), table_ref[c * 256:(c + 1) * 256, :])
        send_part(n, found, send_s, recv_s, rsend, rrecv, 1)
        return carry

    def take(n, carry):
        landed(n, send_s, recv_s, rrecv)
        slab = slabs(n, recv_s)
        for r in range(ROWS // 512):
            at = slice(r * 512, (r + 1) * 512)
            high = high_col[at, :]
            high = jnp.concatenate([high, high], axis=1)
            low = low_col[at, :]
            picked = jnp.concatenate([keep(high == number(2 * n + s, (1, 256)), low) for s in range(2)], axis=1)
            acc_s[at, :] += dot(picked, slab)
        return carry

    lax.fori_loop(0, LEAD, give, 0)
    recv_s[0] = send_s[0]
    low = jnp.broadcast_to(low_ref[...], (128, ROWS)).T
    column = lax.broadcasted_iota(jnp.int32, (ROWS, 128), 1).astype(full)
    low_col[:, :128] = one_hot(low == column)
    low_col[:, 128:] = one_hot(low == column + 128.0)
    high_col[...] = jnp.broadcast_to(high_ref[...], (128, ROWS)).T.astype(half)
    low_row[...] = one_hot(low_ref[...] == lax.broadcasted_iota(jnp.int32, (PART, ROWS), 0).astype(full))
    acc_s[...] = jnp.zeros_like(acc_s)
    aim_s[...] = jnp.broadcast_to(teacher_ref[...], (128, CAND)).T
    out_ref[...] = jnp.zeros_like(out_ref)
    for spare in range(PEERS, PADDED):
        recv_s[spare] = jnp.zeros((CAP, WIDTH), half)
        home_s[spare] = jnp.zeros((CAP, WIDTH), half)
    lax.fori_loop(LEAD, STEPS, lambda n, carry: take(n - LEAD, give(n, carry)), 0)
    lax.fori_loop(STEPS - LEAD, STEPS, take, 0)
    rows_ref[...] = acc_s[...].astype(half)
    for load in loads[1:]:
        load.wait()
    attend(len_ref[0], rows_ref, aim_s, wq_ref, wk_ref, wv_ref, grad_ref, kt_s, vt_s, vk1_s, cq_s, ee_s, xx_s, dvk_s)
    high_row = jnp.broadcast_to(high_ref[...], (16, ROWS))

    def give_back(n, carry):
        found = []
        for s in range(2):
            match = one_hot(high_row == (2 * n + s).astype(full))
            part = jnp.zeros((PART, WIDTH), full)
            for c in range(ROWS // 512):
                at = slice(c * 512, (c + 1) * 512)
                mine = jnp.concatenate([match[:, at]] * (PART // 16), axis=0)
                part = part + dot(mine * low_row[:, at], grad_ref[at, :])
            found.append(part)
        send_part(n, jnp.concatenate(found, axis=0), back_s, home_s, gsend, grecv, -1)
        return carry

    deep = lax.broadcasted_iota(jnp.int32, (256, 512), 0).astype(full)

    def take_back(n, carry):
        landed(n, back_s, home_s, grecv)
        slab = slabs(n, home_s)
        ids = []
        for kk in range(PAIR):
            source = partner(n * PAIR + kk, 1)
            ids.append(asked_ref[source[0], pl.ds(source[1], 1), :][:, :CAP])
            if kk % SUB == SUB - 1:
                ids.append(jnp.zeros((1, 256 - PART), full))
        ids = jnp.concatenate(ids, axis=1)
        high = jnp.floor(ids * (1.0 / 256.0))
        low = one_hot(ids - high * 256.0 == deep)
        high = jnp.broadcast_to(high, (16, 512))
        for c in range(0, TABLE_ROWS // 256, 2):
            picked = []
            for d in range(2):
                mine = one_hot(high == float(c + d))
                picked.append(jnp.concatenate([mine] * 16, axis=0) * low)
            at = slice(c * 256, (c + 2) * 256)
            out_ref[at, :] += dot(jnp.concatenate(picked, axis=0), slab)
        return carry

    lax.fori_loop(0, LAG, give_back, 0)
    home_s[0] = back_s[0]
    lax.fori_loop(LAG, STEPS, lambda n, carry: take_back(n - LAG, give_back(n, carry)), 0)
    lax.fori_loop(STEPS - LAG, STEPS, take_back, 0)
    pltpu.make_async_copy(back_s.at[pl.ds(1, PEERS - 1)], home_s.at[pl.ds(1, PEERS - 1)], gsend).wait()
    pltpu.make_async_copy(item_out.at[pl.ds(1, ITEMS - 1)], item_in.at[pl.ds(1, ITEMS - 1)], isend).wait()
    pltpu.make_async_copy(user_out.at[pl.ds(1, USERS - 1)], asked_ref.at[pl.ds(1, USERS - 1)], usend).wait()
    pltpu.make_async_copy(send_s.at[pl.ds(1, PEERS - 1)], recv_s.at[pl.ds(1, PEERS - 1)], rsend).wait()


def body(cand_ids, hist_ids, hist_len, teacher, table, w_query, w_key, w_value):
    half = jnp.bfloat16
    full = jnp.float32
    space = pl.BlockSpec(memory_space=pltpu.VMEM)
    anywhere = pl.BlockSpec(memory_space=pltpu.HBM)
    sem = pltpu.SemaphoreType.DMA
    vmem = pltpu.VMEM
    return pl.pallas_call(
        ranker_kernel,
        out_shape=pltpu.VMEM((TABLE_ROWS, WIDTH), full),
        in_specs=[pl.BlockSpec(memory_space=pltpu.SMEM)] + [space] * 3 + [anywhere] * 4,
        out_specs=space,
        scratch_shapes=[
            vmem((TABLE_ROWS, WIDTH), half),
            vmem((WIDTH, WIDTH), half),
            vmem((WIDTH, WIDTH), half),
            vmem((WIDTH, WIDTH), half),
            vmem((1, ROWS), full),
            vmem((1, ROWS), full),
            vmem((PEERS, 128), full),
            vmem((ITEMS, USERS, 128), full),
            vmem((ITEMS, USERS, 128), full),
            vmem((USERS, ITEMS, 128), full),
            vmem((USERS, ITEMS, 128), full),
            vmem((PEERS, CAP, 128), full),
            vmem((PADDED, CAP, WIDTH), half),
            vmem((PADDED, CAP, WIDTH), half),
            vmem((PADDED, CAP, WIDTH), half),
            vmem((PADDED, CAP, WIDTH), half),
            vmem((ROWS, 256), half),
            vmem((ROWS, 128), half),
            vmem((PART, ROWS), half),
            vmem((ROWS, WIDTH), full),
            vmem((ROWS, WIDTH), half),
            vmem((ROWS, WIDTH), half),
            vmem((CAND, 128), full),
            vmem((WIDTH, HIST), half),
            vmem((WIDTH, HIST), half),
            vmem((HEADS, HIST, 256), half),
            vmem((HEADS, CAND, 128), half),
            vmem((HEADS, 2 * BLOCK, HIST), half),
            vmem((HEADS, 2 * BLOCK, 128), half),
            vmem((HEADS, 128, HIST), full),
            sem((4,)), sem(()), sem(()), sem(()), sem(()), sem(()), sem((STEPS,)), sem(()), sem((STEPS,)),
        ],
        compiler_params=pltpu.CompilerParams(collective_id=0, has_side_effects=True, vmem_limit_bytes=56 * 2**20),
        name="ranker",
    )(hist_len, cand_ids, hist_ids, teacher, *(pltpu.with_memory_space_constraint(x, pltpu.HBM) for x in (table, w_query, w_key, w_value)))


def solution(mesh):
    placed = (
        P(("user", "item"), None),
        P(("user", "item"), None),
        P(("user", "item")),
        P(("user", "item"), None),
        P(("user", "item"), None),
        P(),
        P(),
        P(),
    )
    return jax.shard_map(
        body, mesh=mesh, in_specs=placed, out_specs=P(("user", "item"), None), check_vma=False
    )
```

```python
import math

import jax
import jax.numpy as jnp
from jax import lax
from jax.experimental import pallas as pl
from jax.experimental.pallas import tpu as pltpu
from jax.sharding import PartitionSpec as P

HEADS = 4
GRAD_SCALE = 1024


CAND = 1024
HIST = 1024
WIDTH = 256
HEAD = 64
BLOCK = 512


def dot(a, b):
    return jnp.dot(a, b, preferred_element_type=jnp.float32)


def dot_tn(a, b):
    return lax.dot_general(a, b, (((0,), (0,)), ((), ())), preferred_element_type=jnp.float32)


def dot_nt(a, b):
    return lax.dot_general(a, b, (((1,), (1,)), ((), ())), preferred_element_type=jnp.float32)


def attend(length, rows_ref, teacher_ref, wq_ref, wk_ref, wv_ref, out_ref, kt_s, vt_s, vk1_s, cq_s, ee_s, xx_s, dvk_s):
    half = jnp.bfloat16
    live = lax.broadcasted_iota(jnp.int32, (HIST, 128), 0) < length
    live2 = jnp.concatenate([live, live], axis=1)
    hist = jnp.where(live2, rows_ref[CAND:, :], jnp.zeros((), half))
    keys = dot(hist, wk_ref[...]).astype(half)
    values = dot(hist, wv_ref[...]).astype(half)
    kt_s[...] = keys.T
    vt_s[...] = values.T
    cand = rows_ref[:CAND, :]
    query = dot(cand, wq_ref[...]).astype(half)
    ones = jnp.where(live, 1.0, 0.0).astype(half)
    for h in range(HEADS):
        part = slice(h * HEAD, (h + 1) * HEAD)
        vk1_s[h] = jnp.concatenate([values[:, part], keys[:, part], ones], axis=1)
        cq_s[h] = jnp.concatenate([cand[:, part], query[:, part]], axis=1)
    dvk_s[...] = jnp.zeros_like(dvk_s)
    first = lax.broadcasted_iota(jnp.int32, (BLOCK, 128), 1) < HEAD
    scale = 1.0 / (math.sqrt(HEAD) * math.log(2.0))

    def step(jb, carry):
        here = pl.ds(pl.multiple_of(jb * BLOCK, BLOCK), BLOCK)
        logit = jnp.zeros((BLOCK, 128), jnp.float32)
        kept = []
        for h in range(HEADS):
            part = slice(h * HEAD, (h + 1) * HEAD)
            cq = cq_s[h, here, :]
            score = dot(cq[:, HEAD:], kt_s[part, :])
            worth = dot(cq[:, :HEAD], vt_s[part, :])
            top = jnp.max(score, axis=1, keepdims=True)
            raised = jnp.exp2((score - top) * scale)
            ee_s[h, :BLOCK, :] = raised.astype(half)
            ee_s[h, BLOCK:, :] = (raised * worth).astype(half)
            both = dot(ee_s[h], vk1_s[h])
            inverse = 1.0 / both[:BLOCK, 128:]
            mean = both[BLOCK:, 128:] * inverse
            plain = both[:BLOCK, :128] * inverse
            lifted = both[BLOCK:, :128] * inverse - mean * plain
            logit = logit + mean
            kept.append((inverse, mean, plain, lifted))
        logit = logit / math.sqrt(WIDTH)
        factor = (GRAD_SCALE / math.sqrt(WIDTH)) * (jax.nn.sigmoid(logit) - jax.nn.sigmoid(teacher_ref[here, :]))
        direct, turned = [], []
        for h in range(HEADS):
            inverse, mean, plain, lifted = kept[h]
            cq = cq_s[h, here, :].astype(jnp.float32)
            weight = factor * inverse
            eighth = weight * (1.0 / math.sqrt(HEAD))
            xx_s[h, :BLOCK, :] = (cq * jnp.where(first, weight, -mean * eighth)).astype(half)
            xx_s[h, BLOCK:, :] = (cq * jnp.where(first, 0.0, eighth)).astype(half)
            dvk_s[h] += dot_tn(xx_s[h], ee_s[h])
            direct.append(plain[:, :HEAD] * factor[:, :HEAD])
            turned.append((lifted[:, HEAD:] * (factor[:, HEAD:] * (1.0 / math.sqrt(HEAD)))))
        back = jnp.concatenate(turned, axis=1).astype(half)
        grad = jnp.concatenate(direct, axis=1) + dot_nt(back, wq_ref[...])
        out_ref[here, :] = grad.astype(half)
        return carry

    lax.fori_loop(0, CAND // BLOCK, step, 0)
    dv = jnp.concatenate([dvk_s[h, :HEAD, :] for h in range(HEADS)], axis=0).astype(half)
    dk = jnp.concatenate([dvk_s[h, HEAD:, :] for h in range(HEADS)], axis=0).astype(half)
    grad_hist = dot_nt(dv.T, wv_ref[...]) + dot_nt(dk.T, wk_ref[...])
    out_ref[CAND:, :] = jnp.where(live2, grad_hist, 0.0).astype(half)


USERS = 16
ITEMS = 8
PEERS = USERS * ITEMS
CAP = 40
TABLE_ROWS = 4096
ROWS = CAND + HIST
SUB = 6
PART = SUB * CAP
PAIR = 2 * SUB
STEPS = 11
PADDED = STEPS * PAIR
LAG = 5
LEAD = 11
MESH = pl.DeviceIdType.MESH


def partner(k, sign):
    dz = k % 4
    dx = (k // 4 + dz) % 4
    dy = (k // 16 + dz) % 4
    dc = k // 64
    user = lax.axis_index("user")
    item = lax.axis_index("item")
    z = (user // 4 + 4 + sign * dz) % 4
    x = (user % 4 + 4 + sign * dx) % 4
    y = (item // 2 + 4 + sign * dy) % 4
    c = (item % 2 + dc) % 2
    return z * 4 + x, y * 2 + c


def partner_index(owner):
    user = lax.axis_index("user")
    item = lax.axis_index("item")
    dz = (user // 4 - owner // 32) & 3
    a = (user % 4 - owner // 8 - dz) & 3
    b = (item // 2 - owner // 2 - dz) & 3
    dc = (item - owner) & 1
    return dc * 64 + b * 16 + a * 4 + dz


def linear(where):
    return where[0] * ITEMS + where[1]


def one_hot(match):
    return jnp.where(match, 1.0, 0.0).astype(jnp.bfloat16)


def keep(match, value):
    return jnp.where(match, value, jnp.zeros((), value.dtype))


def greet():
    user = lax.axis_index("user")
    item = lax.axis_index("item")
    barrier = pltpu.get_barrier_semaphore()
    for step in range(1, ITEMS):
        pl.semaphore_signal(barrier, inc=1, device_id=(user, (item + step) % ITEMS), device_id_type=MESH)
    for step in range(1, USERS):
        pl.semaphore_signal(barrier, inc=1, device_id=((user + step) % USERS, item), device_id_type=MESH)
    return barrier


def requests(cand_ref, hist_ref, high_ref, low_ref):
    half = jnp.bfloat16
    rows = lax.broadcasted_iota(jnp.int32, (PEERS, 256), 0)
    slot = lax.broadcasted_iota(jnp.int32, (64, 256), 0).astype(jnp.float32)
    upper = one_hot(lax.broadcasted_iota(jnp.int32, (256, 256), 0) < lax.broadcasted_iota(jnp.int32, (256, 256), 1))
    taken = jnp.zeros((PEERS, 1), jnp.float32)
    wanted = jnp.zeros((PEERS, 128), jnp.float32)
    for c in range(ROWS // 256):
        at = c * 256
        ids = cand_ref[:, at:at + 256] if at < CAND else hist_ref[:, at - CAND:at - CAND + 256]
        owner = ids // TABLE_ROWS
        local = ids % TABLE_ROWS
        full = jnp.where(rows == owner, 1.0, 0.0)
        chosen = full.astype(half)
        rank = jnp.sum(full * (dot(chosen, upper) + taken), axis=0, keepdims=True)
        taken = taken + jnp.sum(full, axis=1, keepdims=True)
        k = partner_index(owner)
        part = (k * 43) // 256
        high_ref[:, at:at + 256] = part.astype(jnp.float32)
        low_ref[:, at:at + 256] = ((k - part * SUB) * CAP).astype(jnp.float32) + rank
        mine = slot == rank
        upper_half = (local // 64).astype(jnp.float32)
        lower_half = (local % 64).astype(jnp.float32)
        split = jnp.concatenate([jnp.where(mine, upper_half, 0.0), jnp.where(mine, lower_half, 0.0)], axis=0).astype(half)
        wanted = wanted + dot_nt(chosen, split)
    return jnp.concatenate([wanted[:, :64] * 64.0 + wanted[:, 64:], jnp.zeros((PEERS, 64), jnp.float32)], axis=1)


def send_part(n, found, buffer, landing, send_sem, recv_sem, sign, first=0, count=PAIR):
    for kk in range(first, first + count):
        k = n * PAIR + kk
        buffer[k] = found[(kk - first) * CAP:(kk - first + 1) * CAP].astype(jnp.bfloat16)

        def start():
            pltpu.make_async_remote_copy(
                src_ref=buffer.at[k], dst_ref=landing.at[k], send_sem=send_sem, recv_sem=recv_sem.at[n],
                device_id=partner(k, sign), device_id_type=MESH).start()

        if kk == 0:
            pl.when(n > 0)(start)
        elif kk < PEERS - (STEPS - 1) * PAIR:
            start()
        else:
            pl.when(n < STEPS - 1)(start)


def landed(n, buffer, landing, recv_sem):
    def wait(first, count):
        here = pl.ds(first, count)
        pltpu.make_async_copy(buffer.at[here], landing.at[here], recv_sem.at[n]).wait()

    @pl.when(n == 0)
    def _():
        wait(1, PAIR - 1)

    @pl.when(jnp.logical_and(n > 0, n < STEPS - 1))
    def _():
        wait(n * PAIR, PAIR)

    @pl.when(n == STEPS - 1)
    def _():
        wait((STEPS - 1) * PAIR, PEERS - (STEPS - 1) * PAIR)


def slabs(n, landing):
    half = jnp.bfloat16
    tail = jnp.zeros((256 - PART, WIDTH), half)
    parts = []
    for s in range(2):
        part = landing[pl.ds(n * PAIR + s * SUB, SUB)].astype(jnp.float32).reshape(PART, WIDTH).astype(half)
        parts += [part, tail]
    return jnp.concatenate(parts, axis=0)


def number(value, shape):
    return jnp.broadcast_to(jnp.asarray(value, jnp.int32).astype(jnp.float32), shape).astype(jnp.bfloat16)


def ranker_kernel(
    len_ref, cand_ref, hist_ref, teacher_ref, table_any, wq_any, wk_any, wv_any, out_ref,
    table_ref, wq_ref, wk_ref, wv_ref, high_ref, low_ref, want_s, item_out, item_in, user_out, asked_ref, wide_s,
    send_s, recv_s, back_s, home_s, low_col, high_col, low_row, acc_s, rows_ref, grad_ref, aim_s,
    kt_s, vt_s, vk1_s, cq_s, ee_s, xx_s, dvk_s,
    local, isend, irecv, usend, urecv, rsend, rrecv, gsend, grecv,
):
    half = jnp.bfloat16
    full = jnp.float32
    user = lax.axis_index("user")
    item = lax.axis_index("item")
    barrier = greet()
    loads = [
        pltpu.make_async_copy(src, dst, local.at[n])
        for n, (src, dst) in enumerate([(table_any, table_ref), (wq_any, wq_ref), (wk_any, wk_ref), (wv_any, wv_ref)])
    ]
    for load in loads:
        load.start()
    want_s[...] = requests(cand_ref, hist_ref, high_ref, low_ref)
    for i in range(ITEMS):
        item_out[i] = want_s[pl.ds(i, USERS, stride=ITEMS), :]
    pl.semaphore_wait(barrier, USERS + ITEMS - 2)
    for step in range(1, ITEMS):
        to = (item + step) % ITEMS
        pltpu.make_async_remote_copy(
            src_ref=item_out.at[to], dst_ref=item_in.at[item], send_sem=isend, recv_sem=irecv,
            device_id=(user, to), device_id_type=MESH).start()
    item_in[item] = item_out[item]
    pltpu.make_async_copy(item_out.at[pl.ds(1, ITEMS - 1)], item_in.at[pl.ds(1, ITEMS - 1)], irecv).wait()
    for u in range(USERS):
        user_out[u] = jnp.concatenate([item_in[i, u:u + 1, :] for i in range(ITEMS)], axis=0)
    for step in range(1, USERS):
        to = (user + step) % USERS
        pltpu.make_async_remote_copy(
            src_ref=user_out.at[to], dst_ref=asked_ref.at[user], send_sem=usend, recv_sem=urecv,
            device_id=(to, item), device_id_type=MESH).start()
    asked_ref[user] = user_out[user]
    pltpu.make_async_copy(user_out.at[pl.ds(1, USERS - 1)], asked_ref.at[pl.ds(1, USERS - 1)], urecv).wait()
    loads[0].wait()
    turned = asked_ref[...].reshape(PEERS, 128).T
    for p in range(PEERS):
        wide_s[p] = jnp.broadcast_to(turned[:CAP, p:p + 1], (CAP, 128))
    lane = lax.broadcasted_iota(jnp.int32, (2 * PART, 128), 1).astype(full)

    def give(n, carry):
        ids = jnp.concatenate([wide_s[linear(partner(n * PAIR + kk, 1))] for kk in range(PAIR)], axis=0)
        high = jnp.floor(ids * (1.0 / 256.0))
        low = ids - high * 256.0
        low = jnp.concatenate([one_hot(low == lane), one_hot(low == lane + 128.0)], axis=1)
        high = high.astype(half)
        high = jnp.concatenate([high, high], axis=1)
        found = jnp.zeros((2 * PART, WIDTH), full)
        for c in range(TABLE_ROWS // 256):
            found = found + dot(keep(high == number(c, (1, 1)), low), table_ref[c * 256:(c + 1) * 256, :])
        send_part(n, found, send_s, recv_s, rsend, rrecv, 1)
        return carry

    def take(n, carry):
        landed(n, send_s, recv_s, rrecv)
        slab = slabs(n, recv_s)
        for r in range(ROWS // 512):
            at = slice(r * 512, (r + 1) * 512)
            high = high_col[at, :]
            high = jnp.concatenate([high, high], axis=1)
            low = low_col[at, :]
            picked = jnp.concatenate([keep(high == number(2 * n + s, (1, 256)), low) for s in range(2)], axis=1)
            acc_s[at, :] += dot(picked, slab)
        return carry

    lax.fori_loop(0, LEAD, give, 0)
    recv_s[0] = send_s[0]
    low = jnp.broadcast_to(low_ref[...], (128, ROWS)).T
    column = lax.broadcasted_iota(jnp.int32, (ROWS, 128), 1).astype(full)
    low_col[:, :128] = one_hot(low == column)
    low_col[:, 128:] = one_hot(low == column + 128.0)
    high_col[...] = jnp.broadcast_to(high_ref[...], (128, ROWS)).T.astype(half)
    low_row[...] = one_hot(low_ref[...] == lax.broadcasted_iota(jnp.int32, (PART, ROWS), 0).astype(full))
    acc_s[...] = jnp.zeros_like(acc_s)
    aim_s[...] = jnp.broadcast_to(teacher_ref[...], (128, CAND)).T
    out_ref[...] = jnp.zeros_like(out_ref)
    for spare in range(PEERS, PADDED):
        recv_s[spare] = jnp.zeros((CAP, WIDTH), half)
        home_s[spare] = jnp.zeros((CAP, WIDTH), half)
    lax.fori_loop(LEAD, STEPS, lambda n, carry: take(n - LEAD, give(n, carry)), 0)
    lax.fori_loop(STEPS - LEAD, STEPS, take, 0)
    rows_ref[...] = acc_s[...].astype(half)
    for load in loads[1:]:
        load.wait()
    attend(len_ref[0], rows_ref, aim_s, wq_ref, wk_ref, wv_ref, grad_ref, kt_s, vt_s, vk1_s, cq_s, ee_s, xx_s, dvk_s)
    high_row = jnp.broadcast_to(high_ref[...], (16, ROWS))

    def give_back(n, carry):
        for s in range(2):
            match = one_hot(high_row == (2 * n + s).astype(full))
            part = jnp.zeros((PART, WIDTH), full)
            for c in range(ROWS // 512):
                at = slice(c * 512, (c + 1) * 512)
                mine = jnp.concatenate([match[:, at]] * (PART // 16), axis=0)
                part = part + dot(mine * low_row[:, at], grad_ref[at, :])
            send_part(n, part, back_s, home_s, gsend, grecv, -1, s * SUB, SUB)
        return carry

    deep = lax.broadcasted_iota(jnp.int32, (256, 512), 0).astype(full)

    def take_back(n, carry):
        landed(n, back_s, home_s, grecv)
        slab = slabs(n, home_s)
        ids = []
        for kk in range(PAIR):
            source = partner(n * PAIR + kk, 1)
            ids.append(asked_ref[source[0], pl.ds(source[1], 1), :][:, :CAP])
            if kk % SUB == SUB - 1:
                ids.append(jnp.zeros((1, 256 - PART), full))
        ids = jnp.concatenate(ids, axis=1)
        high = jnp.floor(ids * (1.0 / 256.0))
        low = one_hot(ids - high * 256.0 == deep)
        high = jnp.broadcast_to(high, (16, 512))
        for c in range(0, TABLE_ROWS // 256, 2):
            picked = []
            for d in range(2):
                mine = one_hot(high == float(c + d))
                picked.append(jnp.concatenate([mine] * 16, axis=0) * low)
            at = slice(c * 256, (c + 2) * 256)
            out_ref[at, :] += dot(jnp.concatenate(picked, axis=0), slab)
        return carry

    lax.fori_loop(0, LAG, give_back, 0)
    home_s[0] = back_s[0]
    lax.fori_loop(LAG, STEPS, lambda n, carry: take_back(n - LAG, give_back(n, carry)), 0)
    lax.fori_loop(STEPS - LAG, STEPS, take_back, 0)
    pltpu.make_async_copy(back_s.at[pl.ds(1, PEERS - 1)], home_s.at[pl.ds(1, PEERS - 1)], gsend).wait()
    pltpu.make_async_copy(item_out.at[pl.ds(1, ITEMS - 1)], item_in.at[pl.ds(1, ITEMS - 1)], isend).wait()
    pltpu.make_async_copy(user_out.at[pl.ds(1, USERS - 1)], asked_ref.at[pl.ds(1, USERS - 1)], usend).wait()
    pltpu.make_async_copy(send_s.at[pl.ds(1, PEERS - 1)], recv_s.at[pl.ds(1, PEERS - 1)], rsend).wait()


def body(cand_ids, hist_ids, hist_len, teacher, table, w_query, w_key, w_value):
    half = jnp.bfloat16
    full = jnp.float32
    space = pl.BlockSpec(memory_space=pltpu.VMEM)
    anywhere = pl.BlockSpec(memory_space=pltpu.HBM)
    sem = pltpu.SemaphoreType.DMA
    vmem = pltpu.VMEM
    return pl.pallas_call(
        ranker_kernel,
        out_shape=pltpu.VMEM((TABLE_ROWS, WIDTH), full),
        in_specs=[pl.BlockSpec(memory_space=pltpu.SMEM)] + [space] * 3 + [anywhere] * 4,
        out_specs=space,
        scratch_shapes=[
            vmem((TABLE_ROWS, WIDTH), half),
            vmem((WIDTH, WIDTH), half),
            vmem((WIDTH, WIDTH), half),
            vmem((WIDTH, WIDTH), half),
            vmem((1, ROWS), full),
            vmem((1, ROWS), full),
            vmem((PEERS, 128), full),
            vmem((ITEMS, USERS, 128), full),
            vmem((ITEMS, USERS, 128), full),
            vmem((USERS, ITEMS, 128), full),
            vmem((USERS, ITEMS, 128), full),
            vmem((PEERS, CAP, 128), full),
            vmem((PADDED, CAP, WIDTH), half),
            vmem((PADDED, CAP, WIDTH), half),
            vmem((PADDED, CAP, WIDTH), half),
            vmem((PADDED, CAP, WIDTH), half),
            vmem((ROWS, 256), half),
            vmem((ROWS, 128), half),
            vmem((PART, ROWS), half),
            vmem((ROWS, WIDTH), full),
            vmem((ROWS, WIDTH), half),
            vmem((ROWS, WIDTH), half),
            vmem((CAND, 128), full),
            vmem((WIDTH, HIST), half),
            vmem((WIDTH, HIST), half),
            vmem((HEADS, HIST, 256), half),
            vmem((HEADS, CAND, 128), half),
            vmem((HEADS, 2 * BLOCK, HIST), half),
            vmem((HEADS, 2 * BLOCK, 128), half),
            vmem((HEADS, 128, HIST), full),
            sem((4,)), sem(()), sem(()), sem(()), sem(()), sem(()), sem((STEPS,)), sem(()), sem((STEPS,)),
        ],
        compiler_params=pltpu.CompilerParams(collective_id=0, has_side_effects=True, vmem_limit_bytes=56 * 2**20),
        name="ranker",
    )(hist_len, cand_ids, hist_ids, teacher, *(pltpu.with_memory_space_constraint(x, pltpu.HBM) for x in (table, w_query, w_key, w_value)))


def solution(mesh):
    placed = (
        P(("user", "item"), None),
        P(("user", "item"), None),
        P(("user", "item")),
        P(("user", "item"), None),
        P(("user", "item"), None),
        P(),
        P(),
        P(),
    )
    return jax.shard_map(
        body, mesh=mesh, in_specs=placed, out_specs=P(("user", "item"), None), check_vma=False
    )
```
